256 devices in a mesh: expert: 8 (over y, core), row: 8 (over z), col: 4 (over x).
Axes of the slice: x: 4, y: 4, z: 8, core: 2. Of those that a mesh axis runs over, the one named last changes fastest.
Arguments:
- tokens_grad: bfloat16 [1536, 3072], P('expert', ('row', 'col')), may hold values from -2.390625 to 2.390625
- expert_ids: int32 [1536, 2], P('expert'), may hold values from 0 to 7, all different within a row; in each aligned block of 192 rows (0 to 191, 192 to 383, ...) at most 72 rows name the same one
- combine_weights: float32 [1536, 2], P('expert'), may hold values from 0.1 to 1
- gate_saved: bfloat16 [8, 576, 16384], P('expert', None, ('row', 'col')), may hold values from -9 to 9
- up_saved: bfloat16 [8, 576, 16384], P('expert', None, ('row', 'col')), may hold values from -6 to 6
- gate_weight: bfloat16 [8, 3072, 16384], P('expert', None, ('row', 'col')), may hold values from -0.21875 to 0.21875
- up_weight: bfloat16 [8, 3072, 16384], P('expert', None, ('row', 'col')), may hold values from -0.109375 to 0.109375
- down_weight: bfloat16 [8, 16384, 3072], P('expert', ('row', 'col')), may hold values from -0.046875 to 0.046875
Outputs:
- tokens_input_grad: bfloat16 [1536, 3072], P('expert', ('row', 'col'))
The draws below stay inside these ranges and needn't reach their ends.
Inputs may be any that keep to these rules, and one draw needn't show every extreme that they name: `expert_ids`: each token names 2 different experts. Among the 192 tokens of one group no expert is named more than 72 times, and in every draw some group names some expert exactly 72 times.
All inputs are finite; a program needn't handle non-finite values.
Results may differ from the reference program's by a relative error of at most 0.0065.
Values may be sent and summed in bfloat16 or wider, within the bound.
A program may use at most 64 MiB of HBM per device.

```python
import math
import jax
import jax.numpy as jnp
import numpy as np
from jax import lax

D = 3072
FF = 16384
TOP = 2
T_DEV = 192
EXPERTS = 8
CAP = 72
SLOTS = 576
TOKENS = 1536


def strengthened(drawn, key, source, target, shards_of, factor):
    def block_of(axis_at):
        return (jnp.arange(drawn.shape[axis_at]) // (drawn.shape[axis_at] // shards_of)).reshape((-1,) + (1,) * (drawn.ndim - 1 - axis_at))

    one_side = jax.random.permutation(key, shards_of)[block_of(target)]
    other_side = (block_of(target) + shards_of // 2) % shards_of
    return jnp.where((block_of(source) == one_side) | (block_of(source) == other_side), factor * drawn, drawn)


def level_of(rng, dims, cuts, smallest, largest):
    loudness = 1.0
    for dim, shards_of in cuts:
        heights = jax.random.uniform(jax.random.fold_in(jax.random.fold_in(rng, 6), dim), (shards_of,), jnp.float32, smallest / len(cuts), largest / len(cuts))
        loudness = loudness * jnp.repeat(jnp.exp(heights), dims[dim] // shards_of).reshape((-1,) + (1,) * (len(dims) - 1 - dim))
    return loudness


def deal_out(own_key, own, number, rows, number_of, top, most, skew):
    sequence = jax.random.permutation(own_key, number_of)
    packed, ordinary = load_shares(number_of, rows * top, most, skew, True), load_shares(number_of, rows * top, most, skew, False)
    places = jnp.arange(number_of)

    def named(tallies, rotation):
        used = int((tallies > 0).sum())
        fixed = max(1, used // 4)
        passed = fixed + (places - fixed + rotation * (used - fixed)) % max(1, number_of - fixed)
        return jnp.zeros((number_of,), jnp.int32).at[sequence[jnp.where(places < fixed, places, passed)]].set(jnp.asarray(tallies, jnp.int32))

    tallies = jnp.where(number % 4 == 0, named(packed, number // 4), named(ordinary, number - number // 4 - 1))
    mixed = jax.random.permutation(jax.random.fold_in(own, 3), number_of)
    giver, taker = mixed[0:number_of // 2 * 2:2], mixed[1:number_of // 2 * 2:2]
    slack = jnp.minimum(tallies[giver] - 1, most - tallies[taker]) // 2
    slack = jnp.where((giver == sequence[0]) | (taker == sequence[0]) | (tallies[taker] == 0), 0, jnp.maximum(slack, 0))
    passed = jax.random.randint(jax.random.fold_in(own, 4), (number_of // 2,), 0, 1 << 20) % (slack + 1)
    tallies = tallies.at[giver].add(-passed).at[taker].add(passed)
    members = jnp.searchsorted(jnp.cumsum(tallies), jnp.arange(rows * top), side="right").astype(jnp.int32)
    grid = members.reshape(top, rows).T
    grid = grid[jax.random.permutation(jax.random.fold_in(own, 1), rows)]
    rotation = jax.random.randint(jax.random.fold_in(own, 2), (rows, 1), 0, top)
    return jnp.take_along_axis(grid, (jnp.arange(top)[None, :] + rotation) % top, axis=1)


def load_shares(amount, total, limit, skew, full):
    weights = [(1 << 20) // math.isqrt(rank ** skew) + 1 for rank in range(1, amount + 1)]
    largest = limit if full else min(limit, max(-(-total // amount), total * weights[0] // sum(weights)))
    least = 1 if total - largest >= amount - 1 else 0
    counts, surplus = [largest] + [least] * (amount - 1), total - largest - least * (amount - 1)
    while surplus > 0:
        movable = [i for i in range(1, amount) if counts[i] < largest] or [i for i in range(1, amount) if counts[i] < limit]
        pool, remaining = sum([weights[i] for i in movable]), surplus
        for i in movable:
            extra = min(limit - counts[i], max(1, remaining * weights[i] // pool), surplus)
            counts[i] = counts[i] + extra
            surplus = surplus - extra
    return np.array(counts)


def noise(stream_key, dims, deviation, reach, cuts=(), kind=jnp.bfloat16):
    result = deviation * jax.random.normal(stream_key, dims, jnp.float32)
    if cuts:
        result = result * level_of(stream_key, dims, cuts, -0.22, 0.18)
    return jnp.clip(result, -reach, reach).astype(kind)


def bell_draw_with(stream_key, shape, deviation, reach, split, heavy, kind=jnp.bfloat16):
    drawn = deviation * jax.random.normal(stream_key, shape, jnp.float32)
    if split:
        drawn = drawn * level_of(stream_key, shape, split, -0.22, 0.18)
    return jnp.clip(strengthened(drawn, jax.random.fold_in(stream_key, 3), *heavy), -reach, reach).astype(kind)


def setup_inputs(seed: int = 0) -> dict:
    splits = jax.random.split(jax.random.key(seed), 9)
    tokens_grad = noise(splits[0], (TOKENS, D), 0.4, 2.390625, ((0, 8), (1, 32)))
    expert_ids_keys = jax.random.split(jax.random.fold_in(splits[1], 1), TOKENS // T_DEV)
    expert_ids_turns = jax.random.permutation(jax.random.fold_in(splits[1], 3), TOKENS // T_DEV)
    expert_ids = jax.vmap(lambda own, number: deal_out(jax.random.fold_in(splits[1], 2), own, number, T_DEV, EXPERTS, TOP, CAP, 2))(expert_ids_keys, expert_ids_turns).reshape((TOKENS, TOP))
    combine_weights = jnp.clip(0.1 + 0.9 * jax.random.uniform(splits[2], (TOKENS, TOP), jnp.float32) ** level_of(splits[2], (TOKENS, TOP), ((0, 8),), -0.2, 0.2), 0.1, 1.0)
    gate_saved = noise(splits[3], (EXPERTS, SLOTS, FF), 1.5, 9.0, ((0, 8), (2, 32)))
    up_saved = noise(splits[4], (EXPERTS, SLOTS, FF), 1.0, 6.0, ((0, 8), (2, 32)))
    gate_weight = bell_draw_with(splits[5], (EXPERTS, D, FF), D ** -0.5, 0.21875, ((0, 8), (2, 32)), (2, 1, 32, 2.75))
    up_weight = noise(splits[6], (EXPERTS, D, FF), D ** -0.5, 0.109375, ((0, 8), (2, 32)))
    down_weight = noise(splits[7], (EXPERTS, FF, D), FF ** -0.5, 0.046875, ((0, 8), (1, 32)))
    return {"tokens_grad": tokens_grad, "expert_ids": expert_ids, "combine_weights": combine_weights, "gate_saved": gate_saved, "up_saved": up_saved, "gate_weight": gate_weight, "up_weight": up_weight, "down_weight": down_weight}


tanh_scale = 0.7978845608028654
cubic_term = 0.044715


def gelu_pair(pre_act):
    inner_arg = tanh_scale * (pre_act + cubic_term * pre_act * pre_act * pre_act)
    tanh_part = jnp.tanh(inner_arg)
    activation = 0.5 * pre_act * (1.0 + tanh_part)
    derivative = 0.5 * (1.0 + tanh_part) + 0.5 * pre_act * (1.0 - tanh_part * tanh_part) * tanh_scale * (1.0 + 3.0 * cubic_term * pre_act * pre_act)
    return activation, derivative


def group_slots(group_ids):
    flat_ids = group_ids.reshape(-1).astype(jnp.int32)
    onehot = (flat_ids[:, None] == jnp.arange(EXPERTS, dtype=jnp.int32)[None, :]).astype(jnp.int32)
    earlier = jnp.cumsum(onehot, axis=0) - onehot
    position = jnp.sum(earlier * onehot, axis=1)
    return (flat_ids * CAP + position).astype(jnp.int32)


def place_rows(source, slot_row):
    return jnp.zeros((SLOTS, source.shape[1]), source.dtype).at[slot_row].set(source)


def pick_rows(slot_block, slot_row):
    return slot_block[slot_row]


def expert_backward(operands):
    routed_rows, gate_rows, up_rows, gate_mat, up_mat, down_mat = operands
    activation, derivative = gelu_pair(gate_rows.astype(jnp.float32))
    up_float = up_rows.astype(jnp.float32)
    hidden_grad = jnp.dot(routed_rows, down_mat.T, preferred_element_type=jnp.float32)
    gate_grad = (hidden_grad * up_float * derivative).astype(jnp.bfloat16)
    up_grad = (hidden_grad * activation).astype(jnp.bfloat16)
    slot_grad = jnp.dot(gate_grad, gate_mat.T, preferred_element_type=jnp.float32) + jnp.dot(up_grad, up_mat.T, preferred_element_type=jnp.float32)
    return slot_grad.astype(jnp.bfloat16)


def reference(tokens_grad, expert_ids, combine_weights, gate_saved, up_saved, gate_weight, up_weight, down_weight):
    scaled = (combine_weights[:, :, None] * tokens_grad.astype(jnp.float32)[:, None, :]).astype(jnp.bfloat16)
    scaled = scaled.reshape(EXPERTS, T_DEV * TOP, D)
    slot_index = jax.vmap(group_slots)(expert_ids.reshape(EXPERTS, T_DEV, TOP))
    outgoing = jax.vmap(place_rows)(scaled, slot_index)
    routed = outgoing.reshape(EXPERTS, EXPERTS, CAP, D).transpose(1, 0, 2, 3).reshape(EXPERTS, SLOTS, D)
    slot_grads = lax.map(expert_backward, (routed, gate_saved, up_saved, gate_weight, up_weight, down_weight))
    arrived = slot_grads.reshape(EXPERTS, EXPERTS, CAP, D).transpose(1, 0, 2, 3).reshape(EXPERTS, SLOTS, D)
    picked = jax.vmap(pick_rows)(arrived, slot_index)
    picked = picked.astype(jnp.float32).reshape(TOKENS, TOP, D)
    return jnp.sum(picked, axis=1).astype(jnp.bfloat16)
```

```python
import functools

import jax
import jax.numpy as jnp
from jax import lax
from jax.experimental import pallas as pl
from jax.experimental.pallas import tpu as pltpu
from jax.sharding import PartitionSpec as P

tanh_scale = 0.7978845608028654
cubic_term = 0.044715

MESH = pl.DeviceIdType.MESH
F32 = jnp.float32
BF16 = jnp.bfloat16

NE, NZ, NX = 8, 8, 4
CAP = 72
FD = 96
SLAB = NX * FD
HID = 512
CA, CB, CT = 256, 256, 128
NC = CA + CB + CT
HALF = SLAB // 2


def gelu_pair(pre_act):
    inner_arg = tanh_scale * (pre_act + cubic_term * pre_act * pre_act * pre_act)
    tanh_part = jnp.tanh(inner_arg)
    activation = 0.5 * pre_act * (1.0 + tanh_part)
    derivative = 0.5 * (1.0 + tanh_part) + 0.5 * pre_act * (
        1.0 - tanh_part * tanh_part
    ) * tanh_scale * (1.0 + 3.0 * cubic_term * pre_act * pre_act)
    return (activation, derivative)


def mm(a, b):
    return jnp.dot(a, b, preferred_element_type=F32)


def mm_nt(a, b):
    return lax.dot_general(a, b, (((1,), (1,)), ((), ())), preferred_element_type=F32)


def iota(shape, dim):
    return lax.broadcasted_iota(jnp.int32, shape, dim)


def kernel(
    tok_ref, ids_ref, wts_ref, gs_hbm, us_hbm, gw_hbm, uw_hbm, dw_hbm, out_ref,
    gs, us, gw, uw, dw, act_t, dup_t,
    onehot, place, snd1, rcv1, snd2, rcv2,
    xa, xb, xt, xtu, h, gg, ug, slot_t,
    part, sa, sb, st, ra_p, ra_m, rax, sax, rbx, rtx, qb, qt, rbz_p, rbz_m, rtz_p, rtz_m,
    ld, a1s, a1r, a2s, a2r,
    axs, axr, azps, azpr, azms, azmr,
    bzps, bzpr, bzms, bzmr, bxs, bxr,
    rzps, rzpr, rzms, rzmr, rxs, rxr,
    qzps, qzpr, qzms, qzmr, qxs, qxr,
):
    e = lax.axis_index("expert")
    z = lax.axis_index("row")
    x = lax.axis_index("col")

    def dev(de=0, dz=0, dx=0):
        return (
            lax.rem(e + (de + NE), NE),
            lax.rem(z + (dz + NZ), NZ),
            lax.rem(x + (dx + NX), NX),
        )

    def zrel(d):
        return lax.rem(z + (d + NZ), NZ)

    def xrel(d):
        return lax.rem(x + (d + NX), NX)

    def xrows(xx, size):
        return pl.ds(pl.multiple_of(xx * size, size), size)

    started = []

    def send(src, dst, ss, rs, to):
        copy = pltpu.make_async_remote_copy(
            src_ref=src, dst_ref=dst, send_sem=ss, recv_sem=rs, device_id=to, device_id_type=MESH
        )
        copy.start()
        started.append(copy)
        return copy

    loads = [
        pltpu.make_async_copy(gs_hbm.at[0], gs.at[pl.ds(0, 576)], ld.at[0]),
        pltpu.make_async_copy(us_hbm.at[0], us.at[pl.ds(0, 576)], ld.at[1]),
        pltpu.make_async_copy(dw_hbm.at[0], dw, ld.at[2]),
        pltpu.make_async_copy(gw_hbm.at[0], gw, ld.at[3]),
        pltpu.make_async_copy(uw_hbm.at[0], uw, ld.at[4]),
    ]
    for c in loads:
        c.start()
    bar = pltpu.get_barrier_semaphore()
    partners = [dev(de=r) for r in range(1, NE)]
    partners += [dev(dz=1), dev(dz=-1)] + [dev(dx=r) for r in range(1, NX)]
    for p in partners:
        pl.semaphore_signal(bar, inc=1, device_id=p, device_id_type=MESH)

    tok_t = tok_ref[...].astype(F32).T
    ids = ids_ref[...]
    wts = wts_ref[...]
    e_iota = iota((NE, 192), 0)
    first = ids[0:1, :] == e_iota
    second = ids[1:2, :] == e_iota
    named = jnp.where(first, 1.0, jnp.where(second, 1.0, 0.0))
    weight = jnp.where(first, wts[0:1, :], jnp.where(second, wts[1:2, :], 0.0))
    earlier = jnp.where(iota((192, 192), 0) < iota((192, 192), 1), 1.0, 0.0).astype(BF16)
    pos = mm(named.astype(BF16), earlier)
    pos = jnp.where(named > 0.5, pos, -1.0)
    j_iota = iota((128, 192), 0).astype(F32)
    for i in range(NE):
        oh = jnp.where(pos[i : i + 1, :] == j_iota, 1.0, 0.0).astype(BF16)
        onehot[128 * i : 128 * i + 128, :] = oh
        scaled = (tok_t * weight[i : i + 1, :]).astype(BF16)
        snd1[i] = mm_nt(scaled, oh).astype(BF16)

    pl.semaphore_wait(bar, len(partners))

    a2a = {}
    for r in range(1, NE):
        to = lax.rem(e + r, NE)
        a2a[r] = send(snd1.at[to], rcv1.at[e], a1s.at[r], a1r.at[r], dev(de=r))
    rcv1[e] = snd1[e]
    pj = iota((128, NC), 0)
    pc = iota((128, NC), 1)
    for s in range(NE):
        place[128 * s : 128 * s + 128, :] = jnp.where(
            (pc == pj + CAP * s) & (pj < CAP), 1.0, 0.0
        ).astype(BF16)
    gs[576:640, :] = jnp.zeros((64, HID), BF16)
    us[576:640, :] = jnp.zeros((64, HID), BF16)
    h[...] = jnp.zeros_like(h)
    for r in range(1, NE):
        a2a[r].wait_recv()
    rows = mm(rcv1[0], place[0:128, :])
    for s in range(1, NE):
        rows += mm(rcv1[s], place[128 * s : 128 * s + 128, :])
    xa[z, xrows(x, FD), :] = rows[:, :CA].astype(BF16)
    xb[z, xrows(x, FD), :] = rows[:, CA : CA + CB].astype(BF16)
    tail = rows[:, CA + CB :]
    xt[z, xrows(x, FD // 2), :] = (tail[: FD // 2] + pltpu.roll(tail[FD // 2 :], 64, 1)).astype(BF16)

    def gelu_block(b):
        def body(c, carry):
            cols = pl.ds(pl.multiple_of(c * 128, 128), 128)
            act, der = gelu_pair(gs[128 * b : 128 * b + 128, cols].astype(F32))
            der = der * us[128 * b : 128 * b + 128, cols].astype(F32)
            act_t[cols, 128 * b : 128 * b + 128] = act.T
            dup_t[cols, 128 * b : 128 * b + 128] = der.T
            return carry

        lax.fori_loop(0, HID // 128, body, 0)

    def both(k, body):
        if k in (0, 4):
            body(zrel(k))
        else:
            def step(i, carry):
                body(lax.rem(z + NZ + k - 2 * k * i, NZ))
                return carry

            lax.fori_loop(0, 2, step, 0)

    def mm_a(zz):
        cols = pl.ds(pl.multiple_of(zz * SLAB, SLAB), SLAB)
        h[:, :CA] += mm(dw[:, cols], xa[zz])

    def mm_b(zz):
        cols = pl.ds(pl.multiple_of(zz * SLAB, SLAB), SLAB)
        low = iota((FD // 2, 128), 1) < 64
        for i in range(NX):
            t = xt[zz, i * (FD // 2) : (i + 1) * (FD // 2), :].astype(F32)
            xtu[zz, FD * i : FD * i + FD // 2, :] = jnp.where(low, t, 0.0).astype(BF16)
            xtu[zz, FD * i + FD // 2 : FD * i + FD, :] = jnp.where(
                low, pltpu.roll(t, 64, 1), 0.0
            ).astype(BF16)
        h[:, CA : CA + CB] += mm(dw[:, cols], xb[zz])
        h[:, CA + CB :] += mm(dw[:, cols], xtu[zz])

    def bz(zz, to_plus, k):
        ss, rs, to = (bzps, bzpr, dev(dz=1)) if to_plus else (bzms, bzmr, dev(dz=-1))
        m = xb.at[zz, xrows(x, FD)]
        t = xt.at[zz, xrows(x, FD // 2)]
        return (send(m, m, ss.at[0, k], rs.at[0, k], to), send(t, t, ss.at[1, k], rs.at[1, k], to))

    def bx(d, xx, which, dx):
        i = d % NZ
        m = xb.at[zrel(d), xrows(xx, FD)]
        t = xt.at[zrel(d), xrows(xx, FD // 2)]
        to = dev(dx=dx)
        return (
            send(m, m, bxs.at[i, which, 0], bxr.at[i, which, 0], to),
            send(t, t, bxs.at[i, which, 1], bxr.at[i, which, 1], to),
        )

    def got(pair):
        for c in pair:
            c.wait_recv()

    bzp, bzm, bxc, azp, azm = {}, {}, {}, {}, {}
    bzp[0] = bz(z, True, 0)
    bzm[0] = bz(z, False, 0)
    own = xa.at[z, xrows(x, FD)]
    ax = [send(own, own, axs.at[r], axr.at[r], dev(dx=r)) for r in range(1, NX)]

    def bx_first(d):
        bxc[d, 0] = bx(d, x, 0, 1)
        bxc[d, 1] = bx(d, x, 1, -1)

    def bx_second(d):
        if d % 2 == 0:
            got(bxc[d, 0])
            bxc[d, 2] = bx(d, xrel(-1), 2, 1)
        else:
            got(bxc[d, 1])
            bxc[d, 2] = bx(d, xrel(1), 2, -1)

    def bx_done(d):
        got(bxc[d, 1 if d % 2 == 0 else 0])
        got(bxc[d, 2])

    def az(zz, to_plus, k, part_rows=None):
        ss, rs, to = (azps, azpr, dev(dz=1)) if to_plus else (azms, azmr, dev(dz=-1))
        m = xa.at[zz] if part_rows is None else xa.at[zz, part_rows]
        return send(m, m, ss.at[k], rs.at[k], to)

    def ds(k):
        return (k,) if k in (0, 4) else (-k, k)

    bx_first(0)
    for c in loads[:2]:
        c.wait()
    for c in ax:
        c.wait_recv()
    azp[0] = az(z, True, 0)
    azm[0] = az(z, False, 0)
    gelu_block(0)
    loads[2].wait()

    for k in range(1, 5):
        got(bzp[k - 1])
        if k <= 3:
            bzp[k] = bz(zrel(-k), True, k)
            got(bzm[k - 1])
            if k <= 2:
                bzm[k] = bz(zrel(k), False, k)
        for d in ds(k):
            bx_first(d)
        for d in ds(k - 1):
            bx_second(d)
        both(k - 1, mm_a)
        if k >= 2:
            for d in ds(k - 2):
                bx_done(d)
            both(k - 2, mm_b)
        gelu_block(k)
        azp[k - 1].wait_recv()
        if k <= 3:
            azp[k] = az(zrel(-k), True, k, None if k <= 2 else pl.ds(0, HALF))
        azm[k - 1].wait_recv()
        if k <= 3:
            azm[k] = az(zrel(k), False, k, None if k <= 2 else pl.ds(HALF, HALF))
    for d in ds(4):
        bx_second(d)
    both(4, mm_a)
    for d in ds(3):
        bx_done(d)
    both(3, mm_b)
    for d in ds(4):
        bx_done(d)
    both(4, mm_b)

    gg[...] = (h[...] * dup_t[...]).astype(BF16)
    ug[...] = (h[...] * act_t[...]).astype(BF16)
    for c in loads[3:]:
        c.wait()

    def mm_p(zz):
        r = pl.ds(pl.multiple_of(zz * SLAB, SLAB), SLAB)
        p = mm(gw[r, :], gg[...]) + mm(uw[r, :], ug[...])
        part[zz] = p
        sb[zz] = p[:, CA : CA + CB].astype(BF16)
        t = p[:, CA + CB :]
        for i in range(NX):
            st[zz, i * (FD // 2) : (i + 1) * (FD // 2), :] = (
                t[FD * i : FD * i + FD // 2] + pltpu.roll(t[FD * i + FD // 2 : FD * i + FD], 64, 1)
            ).astype(BF16)

    def ra(k, to_plus, rows_):
        zz = zrel(4 - k) if to_plus else zrel(k - 4)
        ss, rs, to, rb = (
            (rzps, rzpr, dev(dz=1), ra_p) if to_plus else (rzms, rzmr, dev(dz=-1), ra_m)
        )
        return send(sa.at[zz, rows_], rb.at[k, rows_], ss.at[k], rs.at[k], to)

    def rx(d, xx, which, dx):
        i = d % NZ
        zz = zrel(d)
        to = dev(dx=dx)
        return (
            send(sb.at[zz, xrows(xx, FD)], rbx.at[i, which], rxs.at[i, which, 0], rxr.at[i, which, 0], to),
            send(st.at[zz, xrows(xx, FD // 2)], rtx.at[i, which], rxs.at[i, which, 1], rxr.at[i, which, 1], to),
        )

    rxc = {}

    def rx_first(d):
        s = 1 if d % 2 == 0 else -1
        rxc[d, 0] = rx(d, xrel(2), 0, s)
        rxc[d, 1] = rx(d, xrel(-s), 1, -s)

    def tail_of(zz, xx):
        base = pl.multiple_of(xx * FD, FD // 2)
        top = part[zz, pl.ds(base, FD // 2), CA + CB :]
        bot = part[zz, pl.ds(pl.multiple_of(base + FD // 2, FD // 2), FD // 2), CA + CB :]
        return top + pltpu.roll(bot, 64, 1)

    def rx_second(d):
        s = 1 if d % 2 == 0 else -1
        i = d % NZ
        zz = zrel(d)
        xx = xrel(s)
        got(rxc[d, 0])
        sb[zz, xrows(xx, FD), :] = (
            part[zz, xrows(xx, FD), CA : CA + CB] + rbx[i, 0].astype(F32)
        ).astype(BF16)
        st[zz, xrows(xx, FD // 2), :] = (tail_of(zz, xx) + rtx[i, 0].astype(F32)).astype(BF16)
        rxc[d, 2] = rx(d, xx, 2, s)

    def rx_done(d):
        i = d % NZ
        zz = zrel(d)
        got(rxc[d, 1])
        got(rxc[d, 2])
        m = part[zz, xrows(x, FD), CA : CA + CB] + rbx[i, 1].astype(F32) + rbx[i, 2].astype(F32)
        t = tail_of(zz, x) + rtx[i, 1].astype(F32) + rtx[i, 2].astype(F32)
        return m, t

    qc = {}

    def q_send(k, to_plus, m, t):
        i = (4 - k) % NZ if to_plus else (k - 4) % NZ
        qb[i] = m.astype(BF16)
        qt[i] = t.astype(BF16)
        ss, rs, to, rb, rt = (
            (qzps, qzpr, dev(dz=1), rbz_p, rtz_p)
            if to_plus
            else (qzms, qzmr, dev(dz=-1), rbz_m, rtz_m)
        )
        qc[k, to_plus] = (
            send(qb.at[i], rb.at[k], ss.at[0, k], rs.at[0, k], to),
            send(qt.at[i], rt.at[k], ss.at[1, k], rs.at[1, k], to),
        )

    def q_stage(k):
        if k == 0:
            m, t = rx_done(4)
            q_send(0, True, m, t)
            return
        m, t = rx_done(4 - k)
        got(qc[k - 1, True])
        q_send(k, True, m + rbz_p[k - 1].astype(F32), t + rtz_p[k - 1].astype(F32))
        m, t = rx_done(k - 4)
        if k >= 2:
            got(qc[k - 1, False])
            m = m + rbz_m[k - 1].astype(F32)
            t = t + rtz_m[k - 1].astype(F32)
        q_send(k, False, m, t)

    rap, ram = {}, {}
    lo, hi, full = pl.ds(0, HALF), pl.ds(HALF, HALF), pl.ds(0, SLAB)
    for k in range(4):
        both(4 - k, mm_p)
        if k == 0:
            sa[zrel(4)] = part[zrel(4), :, :CA].astype(BF16)
            rap[0] = ra(0, True, lo)
            ram[0] = ra(0, False, hi)
        else:
            zp, zm = zrel(4 - k), zrel(k - 4)
            rap[k - 1].wait_recv()
            if k == 1:
                sa[zp, :HALF] = (part[zp, :HALF, :CA] + ra_p[0, :HALF].astype(F32)).astype(BF16)
                sa[zp, HALF:] = part[zp, HALF:, :CA].astype(BF16)
            else:
                sa[zp] = (part[zp, :, :CA] + ra_p[k - 1].astype(F32)).astype(BF16)
            rap[k] = ra(k, True, full)
            ram[k - 1].wait_recv()
            if k == 1:
                sa[zm, :HALF] = part[zm, :HALF, :CA].astype(BF16)
                sa[zm, HALF:] = (part[zm, HALF:, :CA] + ra_m[0, HALF:].astype(F32)).astype(BF16)
            else:
                sa[zm] = (part[zm, :, :CA] + ra_m[k - 1].astype(F32)).astype(BF16)
            ram[k] = ra(k, False, full)
        for d in ds(4 - k):
            rx_first(d)
        if k >= 1:
            for d in ds(5 - k):
                rx_second(d)
        if k >= 2:
            q_stage(k - 2)
    both(0, mm_p)
    rx_first(0)
    for d in ds(1):
        rx_second(d)
    q_stage(2)
    rap[3].wait_recv()
    ram[3].wait_recv()
    part[z, :, :CA] = part[z, :, :CA] + ra_p[3].astype(F32) + ra_m[3].astype(F32)
    sax[...] = part[z, :, :CA].astype(BF16)
    sx = [
        send(sax.at[xrows(xrel(r), FD)], rax.at[r], qxs.at[r], qxr.at[r], dev(dx=r))
        for r in range(1, NX)
    ]
    rx_second(0)
    q_stage(3)
    m, t = rx_done(0)
    for c in sx:
        c.wait_recv()
    a = part[z, xrows(x, FD), :CA]
    for r in range(1, NX):
        a = a + rax[r].astype(F32)
    slot_t[:, :CA] = a.astype(BF16)
    got(qc[3, True])
    got(qc[3, False])
    m = m + rbz_p[3].astype(F32) + rbz_m[3].astype(F32)
    t = t + rtz_p[3].astype(F32) + rtz_m[3].astype(F32)
    slot_t[:, CA : CA + CB] = m.astype(BF16)
    low = iota((FD // 2, 128), 1) < 64
    slot_t[: FD // 2, CA + CB :] = jnp.where(low, t, 0.0).astype(BF16)
    slot_t[FD // 2 :, CA + CB :] = jnp.where(low, pltpu.roll(t, 64, 1), 0.0).astype(BF16)

    for s in range(NE):
        snd2[s] = mm_nt(slot_t[...], place[128 * s : 128 * s + 128, :]).astype(BF16)
    back = {}
    for r in range(1, NE):
        to = lax.rem(e + r, NE)
        back[r] = send(snd2.at[to], rcv2.at[e], a2s.at[r], a2r.at[r], dev(de=r))
    rcv2[e] = snd2[e]
    for r in range(1, NE):
        back[r].wait_recv()
    o = mm(rcv2[0], onehot[0:128, :])
    for s in range(1, NE):
        o += mm(rcv2[s], onehot[128 * s : 128 * s + 128, :])
    out_ref[...] = o.T.astype(BF16)
    for c in started:
        c.wait_send()


def per_device(tokens_grad, expert_ids, combine_weights, gate_saved, up_saved, gate_weight, up_weight, down_weight):
    vmem = pl.BlockSpec(memory_space=pltpu.VMEM)
    hbm = pl.BlockSpec(memory_space=pl.ANY)
    dma = pltpu.SemaphoreType.DMA
    v = pltpu.VMEM
    scratch = [
        v((640, HID), BF16), v((640, HID), BF16),
        v((3072, HID), BF16), v((3072, HID), BF16), v((HID, 3072), BF16),
        v((HID, NC), F32), v((HID, NC), F32),
        v((1024, 192), BF16), v((1024, NC), BF16),
        v((NE, FD, 128), BF16), v((NE, FD, 128), BF16), v((NE, FD, 128), BF16), v((NE, FD, 128), BF16),
        v((NZ, SLAB, CA), BF16), v((NZ, SLAB, CB), BF16), v((NZ, HALF, CT), BF16), v((NZ, SLAB, CT), BF16),
        v((HID, NC), F32), v((HID, NC), BF16), v((HID, NC), BF16), v((FD, NC), BF16),
        v((NZ, SLAB, NC), F32),
        v((NZ, SLAB, CA), BF16), v((NZ, SLAB, CB), BF16), v((NZ, HALF, CT), BF16),
        v((4, SLAB, CA), BF16), v((4, SLAB, CA), BF16),
        v((NX, FD, CA), BF16), v((SLAB, CA), BF16),
        v((NZ, 3, FD, CB), BF16), v((NZ, 3, FD // 2, CT), BF16),
        v((NZ, FD, CB), BF16), v((NZ, FD // 2, CT), BF16),
        v((4, FD, CB), BF16), v((4, FD, CB), BF16), v((4, FD // 2, CT), BF16), v((4, FD // 2, CT), BF16),
        dma((5,)),
        dma((NE,)), dma((NE,)), dma((NE,)), dma((NE,)),
        dma((NX,)), dma((NX,)), dma((4,)), dma((4,)), dma((4,)), dma((4,)),
        dma((2, 4)), dma((2, 4)), dma((2, 4)), dma((2, 4)), dma((NZ, 3, 2)), dma((NZ, 3, 2)),
        dma((4,)), dma((4,)), dma((4,)), dma((4,)), dma((NZ, 3, 2)), dma((NZ, 3, 2)),
        dma((2, 4)), dma((2, 4)), dma((2, 4)), dma((2, 4)), dma((NX,)), dma((NX,)),
    ]
    return pl.pallas_call(
        kernel,
        out_shape=jax.ShapeDtypeStruct(tokens_grad.shape, BF16),
        in_specs=[vmem] * 3 + [hbm] * 5,
        out_specs=vmem,
        scratch_shapes=scratch,
        compiler_params=pltpu.CompilerParams(
            collective_id=0, has_side_effects=True, vmem_limit_bytes=60 * 2**20
        ),
        name="moe_backward",
    )(tokens_grad, expert_ids.T, combine_weights.T, gate_saved, up_saved, gate_weight, up_weight, down_weight)


def solution(mesh):
    in_specs = (
        P("expert", ("row", "col")),
        P("expert", None),
        P("expert", None),
        P("expert", None, ("row", "col")),
        P("expert", None, ("row", "col")),
        P("expert", None, ("row", "col")),
        P("expert", None, ("row", "col")),
        P("expert", ("row", "col"), None),
    )
    out_specs = P("expert", ("row", "col"))
    return jax.shard_map(
        per_device, mesh=mesh, in_specs=in_specs, out_specs=out_specs, check_vma=False
    )
```

```python
import functools

import jax
import jax.numpy as jnp
from jax import lax
from jax.experimental import pallas as pl
from jax.experimental.pallas import tpu as pltpu
from jax.sharding import PartitionSpec as P

tanh_scale = 0.7978845608028654
cubic_term = 0.044715

MESH = pl.DeviceIdType.MESH
F32 = jnp.float32
BF16 = jnp.bfloat16

NE, NZ, NX = 8, 8, 4
CAP = 72
FD = 96
SLAB = NX * FD
HID = 512
CA, CB, CT = 256, 256, 128
NC = CA + CB + CT
HALF = SLAB // 2


def gelu_pair(pre_act):
    inner_arg = tanh_scale * (pre_act + cubic_term * pre_act * pre_act * pre_act)
    tanh_part = jnp.tanh(inner_arg)
    activation = 0.5 * pre_act * (1.0 + tanh_part)
    derivative = 0.5 * (1.0 + tanh_part) + 0.5 * pre_act * (
        1.0 - tanh_part * tanh_part
    ) * tanh_scale * (1.0 + 3.0 * cubic_term * pre_act * pre_act)
    return (activation, derivative)


def mm(a, b):
    return jnp.dot(a, b, preferred_element_type=F32)


def mm_nt(a, b):
    return lax.dot_general(a, b, (((1,), (1,)), ((), ())), preferred_element_type=F32)


def iota(shape, dim):
    return lax.broadcasted_iota(jnp.int32, shape, dim)


def kernel(
    tok_hbm, ids_hbm, wts_hbm, gs_hbm, us_hbm, gw_hbm, uw_hbm, dw_hbm, out_ref,
    tok_ref, ids_ref, wts_ref, gs, us, gw, uw, dw, act_t, dup_t,
    onehot, place, snd1, rcv1, snd2, rcv2,
    xa, xb, xt, xtu, h, gg, ug, slot_t,
    part, sa, sb, st, ra_p, ra_m, rax, sax, rbx, rtx, qb, qt, rbz_p, rbz_m, rtz_p, rtz_m,
    ld, a1s, a1r, a2s, a2r,
    axs, axr, azps, azpr, azms, azmr,
    bzps, bzpr, bzms, bzmr, bxs, bxr,
    rzps, rzpr, rzms, rzmr, rxs, rxr,
    qzps, qzpr, qzms, qzmr, qxs, qxr,
):
    e = lax.axis_index("expert")
    z = lax.axis_index("row")
    x = lax.axis_index("col")

    def dev(de=0, dz=0, dx=0):
        return (
            lax.rem(e + (de + NE), NE),
            lax.rem(z + (dz + NZ), NZ),
            lax.rem(x + (dx + NX), NX),
        )

    def zrel(d):
        return lax.rem(z + (d + NZ), NZ)

    def xrel(d):
        return lax.rem(x + (d + NX), NX)

    def xrows(xx, size):
        return pl.ds(pl.multiple_of(xx * size, size), size)

    started = []

    def send(src, dst, ss, rs, to):
        copy = pltpu.make_async_remote_copy(
            src_ref=src, dst_ref=dst, send_sem=ss, recv_sem=rs, device_id=to, device_id_type=MESH
        )
        copy.start()
        started.append(copy)
        return copy

    bar = pltpu.get_barrier_semaphore()
    partners = [dev(dz=1), dev(dz=-1)] + [dev(dx=r) for r in range(1, NX)]
    partners += [dev(de=r) for r in range(1, NE)]
    for p in partners:
        pl.semaphore_signal(bar, inc=1, device_id=p, device_id_type=MESH)
    small = [
        pltpu.make_async_copy(tok_hbm, tok_ref, ld.at[5]),
        pltpu.make_async_copy(ids_hbm, ids_ref, ld.at[6]),
        pltpu.make_async_copy(wts_hbm, wts_ref, ld.at[7]),
    ]
    loads = [
        pltpu.make_async_copy(gs_hbm.at[0], gs.at[pl.ds(0, 576)], ld.at[0]),
        pltpu.make_async_copy(us_hbm.at[0], us.at[pl.ds(0, 576)], ld.at[1]),
        pltpu.make_async_copy(dw_hbm.at[0], dw, ld.at[2]),
        pltpu.make_async_copy(gw_hbm.at[0], gw, ld.at[3]),
        pltpu.make_async_copy(uw_hbm.at[0], uw, ld.at[4]),
    ]
    for c in small + loads:
        c.start()
    for c in small:
        c.wait()

    tok_t = tok_ref[...].astype(F32).T
    ids = ids_ref[...]
    wts = wts_ref[...]
    e_iota = iota((NE, 192), 0)
    first = ids[0:1, :] == e_iota
    second = ids[1:2, :] == e_iota
    named = jnp.where(first, 1.0, jnp.where(second, 1.0, 0.0))
    weight = jnp.where(first, wts[0:1, :], jnp.where(second, wts[1:2, :], 0.0))
    earlier = jnp.where(iota((192, 192), 0) < iota((192, 192), 1), 1.0, 0.0).astype(BF16)
    pos = mm(named.astype(BF16), earlier)
    pos = jnp.where(named > 0.5, pos, -1.0)
    j_iota = iota((128, 192), 0).astype(F32)
    for i in range(NE):
        oh = jnp.where(pos[i : i + 1, :] == j_iota, 1.0, 0.0).astype(BF16)
        onehot[128 * i : 128 * i + 128, :] = oh
        scaled = (tok_t * weight[i : i + 1, :]).astype(BF16)
        snd1[i] = mm_nt(scaled, oh).astype(BF16)

    pl.semaphore_wait(bar, len(partners))

    a2a = {}
    for r in range(1, NE):
        to = lax.rem(e + r, NE)
        a2a[r] = send(snd1.at[to], rcv1.at[e], a1s.at[r], a1r.at[r], dev(de=r))
    rcv1[e] = snd1[e]
    pj = iota((128, NC), 0)
    pc = iota((128, NC), 1)
    for s in range(NE):
        place[128 * s : 128 * s + 128, :] = jnp.where(
            (pc == pj + CAP * s) & (pj < CAP), 1.0, 0.0
        ).astype(BF16)
    gs[576:640, :] = jnp.zeros((64, HID), BF16)
    us[576:640, :] = jnp.zeros((64, HID), BF16)
    h[...] = jnp.zeros_like(h)
    for r in range(1, NE):
        a2a[r].wait_recv()
    rows = mm(rcv1[0], place[0:128, :])
    for s in range(1, NE):
        rows += mm(rcv1[s], place[128 * s : 128 * s + 128, :])
    xa[z, xrows(x, FD), :] = rows[:, :CA].astype(BF16)
    xb[z, xrows(x, FD), :] = rows[:, CA : CA + CB].astype(BF16)
    tail = rows[:, CA + CB :]
    xt[z, xrows(x, FD // 2), :] = (tail[: FD // 2] + pltpu.roll(tail[FD // 2 :], 64, 1)).astype(BF16)

    def gelu_block(b):
        def body(c, carry):
            cols = pl.ds(pl.multiple_of(c * 128, 128), 128)
            act, der = gelu_pair(gs[128 * b : 128 * b + 128, cols].astype(F32))
            der = der * us[128 * b : 128 * b + 128, cols].astype(F32)
            act_t[cols, 128 * b : 128 * b + 128] = act.T
            dup_t[cols, 128 * b : 128 * b + 128] = der.T
            return carry

        lax.fori_loop(0, HID // 128, body, 0)

    def both(k, body):
        if k in (0, 4):
            body(zrel(k))
        else:
            def step(i, carry):
                body(lax.rem(z + NZ + k - 2 * k * i, NZ))
                return carry

            lax.fori_loop(0, 2, step, 0)

    def mm_a(zz):
        cols = pl.ds(pl.multiple_of(zz * SLAB, SLAB), SLAB)
        h[:, :CA] += mm(dw[:, cols], xa[zz])

    def mm_b(zz):
        cols = pl.ds(pl.multiple_of(zz * SLAB, SLAB), SLAB)
        low = iota((FD // 2, 128), 1) < 64
        for i in range(NX):
            t = xt[zz, i * (FD // 2) : (i + 1) * (FD // 2), :].astype(F32)
            xtu[zz, FD * i : FD * i + FD // 2, :] = jnp.where(low, t, 0.0).astype(BF16)
            xtu[zz, FD * i + FD // 2 : FD * i + FD, :] = jnp.where(
                low, pltpu.roll(t, 64, 1), 0.0
            ).astype(BF16)
        h[:, CA : CA + CB] += mm(dw[:, cols], xb[zz])
        h[:, CA + CB :] += mm(dw[:, cols], xtu[zz])

    def bz(zz, to_plus, k):
        ss, rs, to = (bzps, bzpr, dev(dz=1)) if to_plus else (bzms, bzmr, dev(dz=-1))
        m = xb.at[zz, xrows(x, FD)]
        t = xt.at[zz, xrows(x, FD // 2)]
        return (send(m, m, ss.at[0, k], rs.at[0, k], to), send(t, t, ss.at[1, k], rs.at[1, k], to))

    def bx(d, xx, which, dx):
        i = d % NZ
        m = xb.at[zrel(d), xrows(xx, FD)]
        t = xt.at[zrel(d), xrows(xx, FD // 2)]
        to = dev(dx=dx)
        return (
            send(m, m, bxs.at[i, which, 0], bxr.at[i, which, 0], to),
            send(t, t, bxs.at[i, which, 1], bxr.at[i, which, 1], to),
        )

    def got(pair):
        for c in pair:
            c.wait_recv()

    bzp, bzm, bxc, azp, azm = {}, {}, {}, {}, {}

    def bx_first(d):
        bxc[d, 0] = bx(d, x, 0, 1)
        bxc[d, 1] = bx(d, x, 1, -1)

    def bx_second(d):
        if d % 2 == 0:
            got(bxc[d, 0])
            bxc[d, 2] = bx(d, xrel(-1), 2, 1)
        else:
            got(bxc[d, 1])
            bxc[d, 2] = bx(d, xrel(1), 2, -1)

    def bx_done(d):
        got(bxc[d, 1 if d % 2 == 0 else 0])
        got(bxc[d, 2])

    def az(zz, j, to_plus, k):
        ss, rs, to = (azps, azpr, dev(dz=1)) if to_plus else (azms, azmr, dev(dz=-1))
        m = xa.at[zz, xrows(xrel(j), FD)]
        return send(m, m, ss.at[k, j], rs.at[k, j], to)

    def ds(k):
        return (k,) if k in (0, 4) else (-k, k)

    order = (0, 1, 3, 2)
    plus_last, minus_last = order[:2], order[2:]

    bzp[0] = bz(z, True, 0)
    bzm[0] = bz(z, False, 0)
    azp[0, 0] = az(z, 0, True, 0)
    azm[0, 0] = az(z, 0, False, 0)
    own = xa.at[z, xrows(x, FD)]
    ax = {r: send(own, own, axs.at[r], axr.at[r], dev(dx=r)) for r in (1, 3, 2)}
    bx_first(0)
    for c in loads[:2]:
        c.wait()

    def b_step(k):
        got(bzp[k - 1])
        if k <= 3:
            bzp[k] = bz(zrel(-k), True, k)
            got(bzm[k - 1])
            if k <= 2:
                bzm[k] = bz(zrel(k), False, k)
        for d in ds(k):
            bx_first(d)

    def a_step(k, i):
        jp, jm = order[i], order[i]
        if k == 4:
            jm = order[i + 2]
        azp[k - 1, jp].wait_recv()
        if k <= 2 or (k == 3 and jp in plus_last):
            azp[k, jp] = az(zrel(-k), jp, True, k)
        azm[k - 1, jm].wait_recv()
        if k <= 2 or (k == 3 and jm in minus_last):
            azm[k, jm] = az(zrel(k), jm, False, k)

    def second(k):
        for d in ds(k):
            bx_second(d)

    def done(k):
        for d in ds(k):
            bx_done(d)
        both(k, mm_b)

    for j in order[1:]:
        ax[NX - j].wait_recv()
        azp[0, j] = az(z, j, True, 0)
        azm[0, j] = az(z, j, False, 0)
    b_step(1)
    second(0)
    gelu_block(0)
    a_step(1, 0)
    loads[2].wait()
    both(0, mm_a)
    b_step(2)
    a_step(1, 1)
    gelu_block(1)
    a_step(1, 2)
    second(1)
    a_step(1, 3)
    a_step(2, 0)
    done(0)
    b_step(3)
    both(1, mm_a)
    a_step(2, 1)
    gelu_block(2)
    a_step(2, 2)
    second(2)
    a_step(2, 3)
    done(1)
    b_step(4)
    a_step(3, 0)
    both(2, mm_a)
    a_step(3, 1)
    gelu_block(3)
    a_step(3, 2)
    second(3)
    a_step(3, 3)
    done(2)
    gelu_block(4)
    both(3, mm_a)
    a_step(4, 0)
    second(4)
    a_step(4, 1)
    both(4, mm_a)

    def hidden(cols):
        hh = h[:, cols]
        gg[:, cols] = (hh * dup_t[:, cols]).astype(BF16)
        ug[:, cols] = (hh * act_t[:, cols]).astype(BF16)

    hidden(slice(0, CA))
    for c in loads[3:]:
        c.wait()

    def mm_pa(zz):
        r = pl.ds(pl.multiple_of(zz * SLAB, SLAB), SLAB)
        part[zz, :, :CA] = mm(gw[r, :], gg[:, :CA]) + mm(uw[r, :], ug[:, :CA])

    def mm_pb(zz):
        r = pl.ds(pl.multiple_of(zz * SLAB, SLAB), SLAB)
        p = mm(gw[r, :], gg[:, CA : CA + CB]) + mm(uw[r, :], ug[:, CA : CA + CB])
        part[zz, :, CA : CA + CB] = p
        sb[zz] = p.astype(BF16)
        t = mm(gw[r, :], gg[:, CA + CB :]) + mm(uw[r, :], ug[:, CA + CB :])
        part[zz, :, CA + CB :] = t
        for i in range(NX):
            st[zz, i * (FD // 2) : (i + 1) * (FD // 2), :] = (
                t[FD * i : FD * i + FD // 2] + pltpu.roll(t[FD * i + FD // 2 : FD * i + FD], 64, 1)
            ).astype(BF16)

    rap, ram = {}, {}

    def ra(k, j, to_plus):
        zz = zrel(4 - k) if to_plus else zrel(k - 4)
        ss, rs, to, rb, kept = (
            (rzps, rzpr, dev(dz=1), ra_p, rap) if to_plus else (rzms, rzmr, dev(dz=-1), ra_m, ram)
        )
        r = xrows(xrel(j), FD)
        v = part[zz, r, :CA]
        if (k - 1, j) in kept:
            kept[k - 1, j].wait_recv()
            v = v + rb[k - 1, r].astype(F32)
        sa[zz, r] = v.astype(BF16)
        kept[k, j] = send(sa.at[zz, r], rb.at[k, r], ss.at[k, j], rs.at[k, j], to)

    def rx(d, xx, which, dx):
        i = d % NZ
        zz = zrel(d)
        to = dev(dx=dx)
        return (
            send(sb.at[zz, xrows(xx, FD)], rbx.at[i, which], rxs.at[i, which, 0], rxr.at[i, which, 0], to),
            send(st.at[zz, xrows(xx, FD // 2)], rtx.at[i, which], rxs.at[i, which, 1], rxr.at[i, which, 1], to),
        )

    rxc = {}

    def rx_first(d):
        s = 1 if d % 2 == 0 else -1
        rxc[d, 0] = rx(d, xrel(2), 0, s)
        rxc[d, 1] = rx(d, xrel(-s), 1, -s)

    def tail_of(zz, xx):
        base = pl.multiple_of(xx * FD, FD // 2)
        top = part[zz, pl.ds(base, FD // 2), CA + CB :]
        bot = part[zz, pl.ds(pl.multiple_of(base + FD // 2, FD // 2), FD // 2), CA + CB :]
        return top + pltpu.roll(bot, 64, 1)

    def rx_second(d):
        s = 1 if d % 2 == 0 else -1
        i = d % NZ
        zz = zrel(d)
        xx = xrel(s)
        got(rxc[d, 0])
        sb[zz, xrows(xx, FD), :] = (
            part[zz, xrows(xx, FD), CA : CA + CB] + rbx[i, 0].astype(F32)
        ).astype(BF16)
        st[zz, xrows(xx, FD // 2), :] = (tail_of(zz, xx) + rtx[i, 0].astype(F32)).astype(BF16)
        rxc[d, 2] = rx(d, xx, 2, s)

    def rx_done(d):
        i = d % NZ
        zz = zrel(d)
        got(rxc[d, 1])
        got(rxc[d, 2])
        m = part[zz, xrows(x, FD), CA : CA + CB] + rbx[i, 1].astype(F32) + rbx[i, 2].astype(F32)
        t = tail_of(zz, x) + rtx[i, 1].astype(F32) + rtx[i, 2].astype(F32)
        return m, t

    qc = {}

    def q_send(k, to_plus, m, t):
        i = (4 - k) % NZ if to_plus else (k - 4) % NZ
        qb[i] = m.astype(BF16)
        qt[i] = t.astype(BF16)
        ss, rs, to, rb, rt = (
            (qzps, qzpr, dev(dz=1), rbz_p, rtz_p)
            if to_plus
            else (qzms, qzmr, dev(dz=-1), rbz_m, rtz_m)
        )
        qc[k, to_plus] = (
            send(qb.at[i], rb.at[k], ss.at[0, k], rs.at[0, k], to),
            send(qt.at[i], rt.at[k], ss.at[1, k], rs.at[1, k], to),
        )

    def q_stage(k):
        if k == 0:
            m, t = rx_done(4)
            q_send(0, True, m, t)
            return
        m, t = rx_done(4 - k)
        got(qc[k - 1, True])
        q_send(k, True, m + rbz_p[k - 1].astype(F32), t + rtz_p[k - 1].astype(F32))
        m, t = rx_done(k - 4)
        if k >= 2:
            got(qc[k - 1, False])
            m = m + rbz_m[k - 1].astype(F32)
            t = t + rtz_m[k - 1].astype(F32)
        q_send(k, False, m, t)

    orders_p = ((2, 0), (3, 1, 2, 0), (3, 2, 1, 0), (2, 3, 1, 0))
    orders_m = ((3, 1), (2, 0, 3, 1), (2, 3, 0, 1), (2, 3, 1, 0))

    def ra_both(k, i):
        ra(k, orders_p[k][i], True)
        ra(k, orders_m[k][i], False)

    def firsts(k):
        both(k, mm_pb)
        for d in ds(k):
            rx_first(d)

    def seconds(k):
        for d in ds(k):
            rx_second(d)

    both(4, mm_pa)
    ra_both(0, 0)
    ra_both(0, 1)
    done(3)
    both(3, mm_pa)
    ra_both(1, 0)
    ra_both(1, 1)
    done(4)
    hidden(slice(CA, NC))
    firsts(4)
    ra_both(1, 2)
    ra_both(1, 3)
    firsts(3)
    both(2, mm_pa)
    ra_both(2, 0)
    seconds(4)
    ra_both(2, 1)
    firsts(2)
    seconds(3)
    ra_both(2, 2)
    ra_both(2, 3)
    q_stage(0)
    both(1, mm_pa)
    ra_both(3, 0)
    firsts(1)
    seconds(2)
    ra_both(3, 1)
    ra_both(3, 2)
    q_stage(1)
    firsts(0)
    ra_both(3, 3)
    both(0, mm_pa)
    seconds(1)
    sx = []
    own_a = []

    def final_a(j):
        rap[3, j].wait_recv()
        ram[3, j].wait_recv()
        r = xrows(xrel(j), FD)
        v = part[z, r, :CA] + ra_p[3, r].astype(F32) + ra_m[3, r].astype(F32)
        if j:
            sax[r, :] = v.astype(BF16)
            sx.append(send(sax.at[r], rax.at[j], qxs.at[j], qxr.at[j], dev(dx=j)))
        else:
            own_a.append(v)

    final_a(2)
    q_stage(2)
    final_a(3)
    seconds(0)
    final_a(1)
    q_stage(3)
    final_a(0)
    m, t = rx_done(0)
    got(qc[3, True])
    got(qc[3, False])
    m = m + rbz_p[3].astype(F32) + rbz_m[3].astype(F32)
    t = t + rtz_p[3].astype(F32) + rtz_m[3].astype(F32)
    slot_t[:, CA : CA + CB] = m.astype(BF16)
    low = iota((FD // 2, 128), 1) < 64
    slot_t[: FD // 2, CA + CB :] = jnp.where(low, t, 0.0).astype(BF16)
    slot_t[FD // 2 :, CA + CB :] = jnp.where(low, pltpu.roll(t, 64, 1), 0.0).astype(BF16)
    a = own_a[0]
    for c in sx:
        c.wait_recv()
    for r in range(1, NX):
        a = a + rax[r].astype(F32)
    slot_t[:, :CA] = a.astype(BF16)

    for s in range(NE):
        snd2[s] = mm_nt(slot_t[...], place[128 * s : 128 * s + 128, :]).astype(BF16)
    back = {}
    for r in range(1, NE):
        to = lax.rem(e + r, NE)
        back[r] = send(snd2.at[to], rcv2.at[e], a2s.at[r], a2r.at[r], dev(de=r))
    rcv2[e] = snd2[e]
    for r in range(1, NE):
        back[r].wait_recv()
    o = mm(rcv2[0], onehot[0:128, :])
    for s in range(1, NE):
        o += mm(rcv2[s], onehot[128 * s : 128 * s + 128, :])
    out_ref[...] = o.T.astype(BF16)
    for c in started:
        c.wait_send()


def per_device(tokens_grad, expert_ids, combine_weights, gate_saved, up_saved, gate_weight, up_weight, down_weight):
    vmem = pl.BlockSpec(memory_space=pltpu.VMEM)
    hbm = pl.BlockSpec(memory_space=pl.ANY)
    dma = pltpu.SemaphoreType.DMA
    v = pltpu.VMEM
    scratch = [
        v((192, FD), BF16), v((2, 192), jnp.int32), v((2, 192), F32),
        v((640, HID), BF16), v((640, HID), BF16),
        v((3072, HID), BF16), v((3072, HID), BF16), v((HID, 3072), BF16),
        v((HID, NC), F32), v((HID, NC), F32),
        v((1024, 192), BF16), v((1024, NC), BF16),
        v((NE, FD, 128), BF16), v((NE, FD, 128), BF16), v((NE, FD, 128), BF16), v((NE, FD, 128), BF16),
        v((NZ, SLAB, CA), BF16), v((NZ, SLAB, CB), BF16), v((NZ, HALF, CT), BF16), v((NZ, SLAB, CT), BF16),
        v((HID, NC), F32), v((HID, NC), BF16), v((HID, NC), BF16), v((FD, NC), BF16),
        v((NZ, SLAB, NC), F32),
        v((NZ, SLAB, CA), BF16), v((NZ, SLAB, CB), BF16), v((NZ, HALF, CT), BF16),
        v((4, SLAB, CA), BF16), v((4, SLAB, CA), BF16),
        v((NX, FD, CA), BF16), v((SLAB, CA), BF16),
        v((NZ, 3, FD, CB), BF16), v((NZ, 3, FD // 2, CT), BF16),
        v((NZ, FD, CB), BF16), v((NZ, FD // 2, CT), BF16),
        v((4, FD, CB), BF16), v((4, FD, CB), BF16), v((4, FD // 2, CT), BF16), v((4, FD // 2, CT), BF16),
        dma((8,)),
        dma((NE,)), dma((NE,)), dma((NE,)), dma((NE,)),
        dma((NX,)), dma((NX,)), dma((4, NX)), dma((4, NX)), dma((4, NX)), dma((4, NX)),
        dma((2, 4)), dma((2, 4)), dma((2, 4)), dma((2, 4)), dma((NZ, 3, 2)), dma((NZ, 3, 2)),
        dma((4, NX)), dma((4, NX)), dma((4, NX)), dma((4, NX)), dma((NZ, 3, 2)), dma((NZ, 3, 2)),
        dma((2, 4)), dma((2, 4)), dma((2, 4)), dma((2, 4)), dma((NX,)), dma((NX,)),
    ]
    return pl.pallas_call(
        kernel,
        out_shape=jax.ShapeDtypeStruct(tokens_grad.shape, BF16),
        in_specs=[hbm] * 8,
        out_specs=vmem,
        scratch_shapes=scratch,
        compiler_params=pltpu.CompilerParams(
            collective_id=0, has_side_effects=True, vmem_limit_bytes=60 * 2**20
        ),
        name="moe_backward",
    )(tokens_grad, expert_ids.T, combine_weights.T, gate_saved, up_saved, gate_weight, up_weight, down_weight)


def solution(mesh):
    in_specs = (
        P("expert", ("row", "col")),
        P("expert", None),
        P("expert", None),
        P("expert", None, ("row", "col")),
        P("expert", None, ("row", "col")),
        P("expert", None, ("row", "col")),
        P("expert", None, ("row", "col")),
        P("expert", ("row", "col"), None),
    )
    out_specs = P("expert", ("row", "col"))
    return jax.shard_map(
        per_device, mesh=mesh, in_specs=in_specs, out_specs=out_specs, check_vma=False
    )
```

```python
import math

import jax
import jax.numpy as jnp
from jax import lax
from jax.experimental import pallas as pl
from jax.experimental.pallas import tpu as pltpu
from jax.sharding import PartitionSpec as P

tanh_scale = 0.7978845608028654
cubic_term = 0.044715

MESH = pl.DeviceIdType.MESH
F32 = jnp.float32
BF16 = jnp.bfloat16

NE, NZ, NX = 8, 8, 4
CAP = 72
FD = 96
SLAB = NX * FD
HID = 512
CA, CB, CT = 256, 256, 128
NC = CA + CB + CT
HALF = SLAB // 2


def gelu_pair(pre_act):
    inner_arg = tanh_scale * (pre_act + cubic_term * pre_act * pre_act * pre_act)
    tanh_part = jnp.tanh(inner_arg)
    activation = 0.5 * pre_act * (1.0 + tanh_part)
    derivative = 0.5 * (1.0 + tanh_part) + 0.5 * pre_act * (
        1.0 - tanh_part * tanh_part
    ) * tanh_scale * (1.0 + 3.0 * cubic_term * pre_act * pre_act)
    return (activation, derivative)


def mm(a, b):
    return jnp.dot(a, b, preferred_element_type=F32)


def mm_nt(a, b):
    return lax.dot_general(a, b, (((1,), (1,)), ((), ())), preferred_element_type=F32)


def iota(shape, dim):
    return lax.broadcasted_iota(jnp.int32, shape, dim)


def kernel(
    tok_hbm, ids_hbm, wts_hbm, gs_hbm, us_hbm, gw_hbm, uw_hbm, dw_hbm, out_ref,
    tok_ref, ids_ref, wts_ref, gs, us, gw, uw, dw, act_t, dup_t,
    onehot, pos_ref, weight_ref, snd1, rcv1, snd2, rcv2,
    xa, xb, xt, xtu, h, gg, ug,
    part, sa, sb, st, ra_p, ra_m, rax, sax, rbx, rtx, qb, qt, rbz_p, rbz_m, rtz_p, rtz_m,
    size_ref, sent, ld, a1r, a2r, axr, azpr, azmr, bzpr, bzmr, bxr, rzpr, rzmr, rxr, qzpr, qzmr, qxr,
):
    e = lax.axis_index("expert")
    z = lax.axis_index("row")
    x = lax.axis_index("col")

    def dev(de=0, dz=0, dx=0):
        return (
            lax.rem(e + (de + NE), NE),
            lax.rem(z + (dz + NZ), NZ),
            lax.rem(x + (dx + NX), NX),
        )

    def zrel(d):
        return lax.rem(z + (d + NZ), NZ)

    def xrel(d):
        return lax.rem(x + (d + NX), NX)

    def xrows(xx, size):
        return pl.ds(pl.multiple_of(xx * size, size), size)

    sent_bytes = [0, 0, 0, 0]

    def send(phase, src, dst, rs, to):
        copy = pltpu.make_async_remote_copy(
            src_ref=src, dst_ref=dst, send_sem=sent.at[phase], recv_sem=rs, device_id=to, device_id_type=MESH
        )
        copy.start()
        sent_bytes[phase] += 2 * math.prod(src.shape)
        return copy

    def wait_bytes(sem, size):
        whole = size_ref.at[pl.ds(0, size // 512)]
        pltpu.make_async_copy(whole, whole, sem).wait()

    def got(sem):
        wait_bytes(sem, 2 * FD * (CB + CT // 2))

    bar = pltpu.get_barrier_semaphore()
    partners = [dev(dz=1), dev(dz=-1)] + [dev(dx=r) for r in range(1, NX)]
    partners += [dev(de=r) for r in range(1, NE)]
    for p in partners:
        pl.semaphore_signal(bar, inc=1, device_id=p, device_id_type=MESH)
    small = [
        pltpu.make_async_copy(tok_hbm, tok_ref, ld.at[5]),
        pltpu.make_async_copy(ids_hbm, ids_ref, ld.at[6]),
        pltpu.make_async_copy(wts_hbm, wts_ref, ld.at[7]),
    ]
    loads = [
        pltpu.make_async_copy(gs_hbm.at[0], gs.at[pl.ds(0, 576)], ld.at[0]),
        pltpu.make_async_copy(us_hbm.at[0], us.at[pl.ds(0, 576)], ld.at[1]),
        pltpu.make_async_copy(dw_hbm.at[0], dw, ld.at[2]),
        pltpu.make_async_copy(gw_hbm.at[0], gw, ld.at[3]),
        pltpu.make_async_copy(uw_hbm.at[0], uw, ld.at[4]),
    ]
    for c in small + loads:
        c.start()
    for c in small:
        c.wait()

    tok_t = tok_ref[...].astype(F32).T
    ids = ids_ref[...]
    wts = wts_ref[...]
    e_iota = iota((NE, 192), 0)
    first = ids[0:1, :] == e_iota
    second = ids[1:2, :] == e_iota
    named = jnp.where(first, 1.0, jnp.where(second, 1.0, 0.0))
    weight = jnp.where(first, wts[0:1, :], jnp.where(second, wts[1:2, :], 0.0))
    earlier = jnp.where(iota((192, 192), 0) < iota((192, 192), 1), 1.0, 0.0).astype(BF16)
    pos = mm(named.astype(BF16), earlier)
    pos_ref[...] = jnp.where(named > 0.5, pos, -1.0)
    weight_ref[...] = weight
    j_iota = iota((128, 192), 0).astype(F32)
    lane = iota((FD, 128), 1)
    far_first = (4, 3, 5, 2, 6, 1, 7)

    def dispatch(i):
        oh = jnp.where(pos_ref[pl.ds(i, 1), :] == j_iota, 1.0, 0.0).astype(BF16)
        onehot[i] = oh
        scaled = (tok_t * weight_ref[pl.ds(i, 1), :]).astype(BF16)
        return mm_nt(scaled, oh).astype(BF16)

    pl.semaphore_wait(bar, len(partners))

    a2a = {}
    for r in far_first:
        to = lax.rem(e + r, NE)
        snd1[to] = dispatch(to)
        a2a[r] = send(0, snd1.at[to], rcv1.at[e], a1r.at[r], dev(de=r))
    rcv1[e] = dispatch(e)
    gs[576:640, :] = jnp.zeros((64, HID), BF16)
    us[576:640, :] = jnp.zeros((64, HID), BF16)
    h[...] = jnp.zeros_like(h)
    for r in far_first:
        a2a[r].wait_recv()
    tiles = [jnp.zeros((FD, 128), F32) for _ in range(NC // 128)]
    for s in range(NE):
        q, shift = divmod(CAP * s, 128)
        block = rcv1[s].astype(F32)
        if shift:
            block = pltpu.roll(block, shift, 1)
        if shift + CAP <= 128:
            tiles[q] += block
        else:
            tiles[q] += jnp.where(lane >= shift, block, 0.0)
            tiles[q + 1] += jnp.where(lane < shift, block, 0.0)
    tiles = [t.astype(BF16) for t in tiles]
    xb[z, xrows(x, FD), :128] = tiles[2]
    xb[z, xrows(x, FD), 128:] = tiles[3]
    tail = tiles[4].astype(F32)
    xt[z, xrows(x, FD // 2), :] = (tail[: FD // 2] + pltpu.roll(tail[FD // 2 :], 64, 1)).astype(BF16)
    xa[z, xrows(x, FD), :128] = tiles[0]
    xa[z, xrows(x, FD), 128:] = tiles[1]

    def gelu_block(b):
        def body(c, carry):
            cols = pl.ds(pl.multiple_of(c * 128, 128), 128)
            act, der = gelu_pair(gs[128 * b : 128 * b + 128, cols].astype(F32))
            der = der * us[128 * b : 128 * b + 128, cols].astype(F32)
            act_t[cols, 128 * b : 128 * b + 128] = act.T
            dup_t[cols, 128 * b : 128 * b + 128] = der.T
            return carry

        lax.fori_loop(0, HID // 128, body, 0)

    def both(k, body):
        if k in (0, 4):
            body(zrel(k))
        else:
            def step(i, carry):
                body(lax.rem(z + NZ + k - 2 * k * i, NZ))
                return carry

            lax.fori_loop(0, 2, step, 0)

    def mm_a(zz):
        cols = pl.ds(pl.multiple_of(zz * SLAB, SLAB), SLAB)
        h[:, :CA] += mm(dw[:, cols], xa[zz])

    def mm_b(zz):
        cols = pl.ds(pl.multiple_of(zz * SLAB, SLAB), SLAB)
        low = iota((FD // 2, 128), 1) < 64
        for i in range(NX):
            t = xt[zz, i * (FD // 2) : (i + 1) * (FD // 2), :].astype(F32)
            xtu[zz, FD * i : FD * i + FD // 2, :] = jnp.where(low, t, 0.0).astype(BF16)
            xtu[zz, FD * i + FD // 2 : FD * i + FD, :] = jnp.where(
                low, pltpu.roll(t, 64, 1), 0.0
            ).astype(BF16)
        h[:, CA : CA + CB] += mm(dw[:, cols], xb[zz])
        h[:, CA + CB :] += mm(dw[:, cols], xtu[zz])

    def bz(zz, to_plus, k):
        rs, to = (bzpr, dev(dz=1)) if to_plus else (bzmr, dev(dz=-1))
        for buf, size in ((xb, FD), (xt, FD // 2)):
            m = buf.at[zz, xrows(x, size)]
            send(1, m, m, rs.at[k], to)
        return rs.at[k]

    def bx(d, xx, which, dx):
        sem = bxr.at[d % NZ, which]
        for buf, size in ((xb, FD), (xt, FD // 2)):
            m = buf.at[zrel(d), xrows(xx, size)]
            send(1, m, m, sem, dev(dx=dx))
        return sem

    bzp, bzm, bxc, azp, azm = {}, {}, {}, {}, {}

    def bx_first(d):
        bxc[d, 0] = bx(d, x, 0, 1)
        bxc[d, 1] = bx(d, x, 1, -1)

    def bx_second(d):
        if d % 2 == 0:
            got(bxc[d, 0])
            bxc[d, 2] = bx(d, xrel(-1), 2, 1)
        else:
            got(bxc[d, 1])
            bxc[d, 2] = bx(d, xrel(1), 2, -1)

    def bx_done(d):
        got(bxc[d, 1 if d % 2 == 0 else 0])
        got(bxc[d, 2])

    def az(zz, j, to_plus, k):
        rs, to = (azpr, dev(dz=1)) if to_plus else (azmr, dev(dz=-1))
        m = xa.at[zz, xrows(xrel(j), FD)]
        return send(1, m, m, rs.at[k, j], to)

    def ds(k):
        return (k,) if k in (0, 4) else (-k, k)

    order = (0, 1, 3, 2)
    plus_last, minus_last = order[:2], order[2:]

    bzp[0] = bz(z, True, 0)
    bzm[0] = bz(z, False, 0)
    azp[0, 0] = az(z, 0, True, 0)
    azm[0, 0] = az(z, 0, False, 0)
    own = xa.at[z, xrows(x, FD)]
    ax = {r: send(1, own, own, axr.at[r], dev(dx=r)) for r in (1, 3, 2)}
    bx_first(0)
    for c in loads[:2]:
        c.wait()

    def b_step(k):
        got(bzp[k - 1])
        if k <= 3:
            bzp[k] = bz(zrel(-k), True, k)
            got(bzm[k - 1])
            if k <= 2:
                bzm[k] = bz(zrel(k), False, k)
        for d in ds(k):
            bx_first(d)

    def a_step(k, i):
        jp, jm = order[i], order[i]
        if k == 4:
            jm = order[i + 2]
        azp[k - 1, jp].wait_recv()
        if k <= 2 or (k == 3 and jp in plus_last):
            azp[k, jp] = az(zrel(-k), jp, True, k)
        azm[k - 1, jm].wait_recv()
        if k <= 2 or (k == 3 and jm in minus_last):
            azm[k, jm] = az(zrel(k), jm, False, k)

    def second(k):
        for d in ds(k):
            bx_second(d)

    def done(k):
        for d in ds(k):
            bx_done(d)
        both(k, mm_b)

    for j in order[1:]:
        ax[NX - j].wait_recv()
        azp[0, j] = az(z, j, True, 0)
        azm[0, j] = az(z, j, False, 0)
    b_step(1)
    second(0)
    gelu_block(0)
    a_step(1, 0)
    loads[2].wait()
    both(0, mm_a)
    b_step(2)
    a_step(1, 1)
    gelu_block(1)
    a_step(1, 2)
    second(1)
    a_step(1, 3)
    a_step(2, 0)
    done(0)
    b_step(3)
    both(1, mm_a)
    a_step(2, 1)
    gelu_block(2)
    a_step(2, 2)
    second(2)
    a_step(2, 3)
    done(1)
    b_step(4)
    a_step(3, 0)
    both(2, mm_a)
    a_step(3, 1)
    gelu_block(3)
    a_step(3, 2)
    second(3)
    a_step(3, 3)
    done(2)
    gelu_block(4)
    both(3, mm_a)
    a_step(4, 0)
    second(4)
    a_step(4, 1)
    both(4, mm_a)

    def hidden(cols):
        hh = h[:, cols]
        gg[:, cols] = (hh * dup_t[:, cols]).astype(BF16)
        ug[:, cols] = (hh * act_t[:, cols]).astype(BF16)

    hidden(slice(0, CA))
    for c in loads[3:]:
        c.wait()

    def mm_pa(zz):
        r = pl.ds(pl.multiple_of(zz * SLAB, SLAB), SLAB)
        part[zz, :, :CA] = mm(gw[r, :], gg[:, :CA]) + mm(uw[r, :], ug[:, :CA])

    def mm_pb(zz):
        r = pl.ds(pl.multiple_of(zz * SLAB, SLAB), SLAB)
        p = mm(gw[r, :], gg[:, CA : CA + CB]) + mm(uw[r, :], ug[:, CA : CA + CB])
        part[zz, :, CA : CA + CB] = p
        sb[zz] = p.astype(BF16)
        t = mm(gw[r, :], gg[:, CA + CB :]) + mm(uw[r, :], ug[:, CA + CB :])
        part[zz, :, CA + CB :] = t
        for i in range(NX):
            st[zz, i * (FD // 2) : (i + 1) * (FD // 2), :] = (
                t[FD * i : FD * i + FD // 2] + pltpu.roll(t[FD * i + FD // 2 : FD * i + FD], 64, 1)
            ).astype(BF16)

    rap, ram = {}, {}

    def ra(k, j, to_plus):
        zz = zrel(4 - k) if to_plus else zrel(k - 4)
        rs, to, rb, kept = (rzpr, dev(dz=1), ra_p, rap) if to_plus else (rzmr, dev(dz=-1), ra_m, ram)
        r = xrows(xrel(j), FD)
        v = part[zz, r, :CA]
        if (k - 1, j) in kept:
            kept[k - 1, j].wait_recv()
            v = v + rb[k - 1, r].astype(F32)
        sa[zz, r] = v.astype(BF16)
        kept[k, j] = send(2, sa.at[zz, r], rb.at[k, r], rs.at[k, j], to)

    def rx(d, xx, which, dx):
        i = d % NZ
        zz = zrel(d)
        sem = rxr.at[i, which]
        send(2, sb.at[zz, xrows(xx, FD)], rbx.at[i, which], sem, dev(dx=dx))
        send(2, st.at[zz, xrows(xx, FD // 2)], rtx.at[i, which], sem, dev(dx=dx))
        return sem

    rxc = {}

    def rx_first(d):
        s = 1 if d % 2 == 0 else -1
        rxc[d, 0] = rx(d, xrel(2), 0, s)
        rxc[d, 1] = rx(d, xrel(-s), 1, -s)

    def tail_of(zz, xx):
        base = pl.multiple_of(xx * FD, FD // 2)
        top = part[zz, pl.ds(base, FD // 2), CA + CB :]
        bot = part[zz, pl.ds(pl.multiple_of(base + FD // 2, FD // 2), FD // 2), CA + CB :]
        return top + pltpu.roll(bot, 64, 1)

    def rx_second(d):
        s = 1 if d % 2 == 0 else -1
        i = d % NZ
        zz = zrel(d)
        xx = xrel(s)
        got(rxc[d, 0])
        sb[zz, xrows(xx, FD), :] = (
            part[zz, xrows(xx, FD), CA : CA + CB] + rbx[i, 0].astype(F32)
        ).astype(BF16)
        st[zz, xrows(xx, FD // 2), :] = (tail_of(zz, xx) + rtx[i, 0].astype(F32)).astype(BF16)
        rxc[d, 2] = rx(d, xx, 2, s)

    def rx_done(d):
        i = d % NZ
        zz = zrel(d)
        got(rxc[d, 1])
        got(rxc[d, 2])
        m = part[zz, xrows(x, FD), CA : CA + CB] + rbx[i, 1].astype(F32) + rbx[i, 2].astype(F32)
        t = tail_of(zz, x) + rtx[i, 1].astype(F32) + rtx[i, 2].astype(F32)
        return m, t

    qc = {}

    def q_send(k, to_plus, m, t):
        i = (4 - k) % NZ if to_plus else (k - 4) % NZ
        qb[i] = m.astype(BF16)
        qt[i] = t.astype(BF16)
        rs, to, rb, rt = (
            (qzpr, dev(dz=1), rbz_p, rtz_p) if to_plus else (qzmr, dev(dz=-1), rbz_m, rtz_m)
        )
        send(2, qb.at[i], rb.at[k], rs.at[k], to)
        send(2, qt.at[i], rt.at[k], rs.at[k], to)
        qc[k, to_plus] = rs.at[k]

    def q_stage(k):
        if k == 0:
            m, t = rx_done(4)
            q_send(0, True, m, t)
            return
        m, t = rx_done(4 - k)
        got(qc[k - 1, True])
        q_send(k, True, m + rbz_p[k - 1].astype(F32), t + rtz_p[k - 1].astype(F32))
        m, t = rx_done(k - 4)
        if k >= 2:
            got(qc[k - 1, False])
            m = m + rbz_m[k - 1].astype(F32)
            t = t + rtz_m[k - 1].astype(F32)
        q_send(k, False, m, t)

    orders_p = ((2, 0), (3, 1, 2, 0), (3, 2, 1, 0), (2, 3, 1, 0))
    orders_m = ((3, 1), (2, 0, 3, 1), (2, 3, 0, 1), (2, 3, 1, 0))

    def ra_both(k, i):
        ra(k, orders_p[k][i], True)
        ra(k, orders_m[k][i], False)

    def firsts(k):
        both(k, mm_pb)
        for d in ds(k):
            rx_first(d)

    def seconds(k):
        for d in ds(k):
            rx_second(d)

    both(4, mm_pa)
    ra_both(0, 0)
    ra_both(0, 1)
    done(3)
    both(3, mm_pa)
    ra_both(1, 0)
    ra_both(1, 1)
    done(4)
    hidden(slice(CA, NC))
    firsts(4)
    ra_both(1, 2)
    ra_both(1, 3)
    firsts(3)
    both(2, mm_pa)
    ra_both(2, 0)
    seconds(4)
    ra_both(2, 1)
    firsts(2)
    seconds(3)
    ra_both(2, 2)
    ra_both(2, 3)
    q_stage(0)
    both(1, mm_pa)
    ra_both(3, 0)
    firsts(1)
    seconds(2)
    ra_both(3, 1)
    ra_both(3, 2)
    q_stage(1)
    firsts(0)
    ra_both(3, 3)
    both(0, mm_pa)
    seconds(1)
    sx = []
    own_a = []

    def final_a(j):
        rap[3, j].wait_recv()
        ram[3, j].wait_recv()
        r = xrows(xrel(j), FD)
        v = part[z, r, :CA] + ra_p[3, r].astype(F32) + ra_m[3, r].astype(F32)
        if j:
            sax[r, :] = v.astype(BF16)
            sx.append(send(2, sax.at[r], rax.at[j], qxr.at[j], dev(dx=j)))
        else:
            own_a.append(v)

    final_a(2)
    q_stage(2)
    final_a(3)
    seconds(0)
    final_a(1)
    q_stage(3)
    final_a(0)
    m, t = rx_done(0)
    got(qc[3, True])
    got(qc[3, False])
    m = m + rbz_p[3].astype(F32) + rbz_m[3].astype(F32)
    t = t + rtz_p[3].astype(F32) + rtz_m[3].astype(F32)
    low = iota((FD // 2, 128), 1) < 64
    t = jnp.concatenate([jnp.where(low, t, 0.0), jnp.where(low, pltpu.roll(t, 64, 1), 0.0)], axis=0)
    a = own_a[0]
    for c in sx:
        c.wait_recv()
    for r in range(1, NX):
        a = a + rax[r].astype(F32)

    tiles = [v.astype(BF16).astype(F32) for v in (a[:, :128], a[:, 128:], m[:, :128], m[:, 128:], t)]
    for s in range(NE):
        q, shift = divmod(CAP * s, 128)
        block = tiles[q]
        if shift + CAP > 128:
            block = jnp.where(lane >= shift, block, tiles[q + 1])
        if shift:
            block = pltpu.roll(block, 128 - shift, 1)
        snd2[s] = block.astype(BF16)
    back = {}
    for r in far_first:
        to = lax.rem(e + r, NE)
        back[r] = send(3, snd2.at[to], rcv2.at[e], a2r.at[r], dev(de=r))
    o = mm(snd2[e], onehot[e])
    for r in (1, 7, 2, 6, 3, 5, 4):
        back[r].wait_recv()
        i = lax.rem(e + NE - r, NE)
        o += mm(rcv2[i], onehot[i])
    out_ref[...] = o.T.astype(BF16)
    for phase, size in enumerate(sent_bytes):
        wait_bytes(sent.at[phase], size)


def per_device(tokens_grad, expert_ids, combine_weights, gate_saved, up_saved, gate_weight, up_weight, down_weight):
    vmem = pl.BlockSpec(memory_space=pltpu.VMEM)
    hbm = pl.BlockSpec(memory_space=pl.ANY)
    dma = pltpu.SemaphoreType.DMA
    v = pltpu.VMEM
    scratch = [
        v((192, FD), BF16), v((2, 192), jnp.int32), v((2, 192), F32),
        v((640, HID), BF16), v((640, HID), BF16),
        v((3072, HID), BF16), v((3072, HID), BF16), v((HID, 3072), BF16),
        v((HID, NC), F32), v((HID, NC), F32),
        v((NE, 128, 192), BF16), v((NE, 192), F32), v((NE, 192), F32),
        v((NE, FD, 128), BF16), v((NE, FD, 128), BF16), v((NE, FD, 128), BF16), v((NE, FD, 128), BF16),
        v((NZ, SLAB, CA), BF16), v((NZ, SLAB, CB), BF16), v((NZ, HALF, CT), BF16), v((NZ, SLAB, CT), BF16),
        v((HID, NC), F32), v((HID, NC), BF16), v((HID, NC), BF16),
        v((NZ, SLAB, NC), F32),
        v((NZ, SLAB, CA), BF16), v((NZ, SLAB, CB), BF16), v((NZ, HALF, CT), BF16),
        v((4, SLAB, CA), BF16), v((4, SLAB, CA), BF16),
        v((NX, FD, CA), BF16), v((SLAB, CA), BF16),
        v((NZ, 3, FD, CB), BF16), v((NZ, 3, FD // 2, CT), BF16),
        v((NZ, FD, CB), BF16), v((NZ, FD // 2, CT), BF16),
        v((4, FD, CB), BF16), v((4, FD, CB), BF16), v((4, FD // 2, CT), BF16), v((4, FD // 2, CT), BF16),
        v((6720, 128), F32),
        dma((4,)), dma((8,)), dma((NE,)), dma((NE,)),
        dma((NX,)), dma((4, NX)), dma((4, NX)), dma((4,)), dma((3,)), dma((NZ, 3)),
        dma((4, NX)), dma((4, NX)), dma((NZ, 3)), dma((4,)), dma((4,)), dma((NX,)),
    ]
    return pl.pallas_call(
        kernel,
        out_shape=jax.ShapeDtypeStruct(tokens_grad.shape, BF16),
        in_specs=[hbm] * 8,
        out_specs=vmem,
        scratch_shapes=scratch,
        compiler_params=pltpu.CompilerParams(
            collective_id=0, has_side_effects=True, vmem_limit_bytes=60 * 2**20
        ),
        name="moe_backward",
    )(tokens_grad, expert_ids.T, combine_weights.T, gate_saved, up_saved, gate_weight, up_weight, down_weight)


def solution(mesh):
    in_specs = (
        P("expert", ("row", "col")),
        P("expert", None),
        P("expert", None),
        P("expert", None, ("row", "col")),
        P("expert", None, ("row", "col")),
        P("expert", None, ("row", "col")),
        P("expert", None, ("row", "col")),
        P("expert", ("row", "col"), None),
    )
    out_specs = P("expert", ("row", "col"))
    return jax.shard_map(
        per_device, mesh=mesh, in_specs=in_specs, out_specs=out_specs, check_vma=False
    )
```

```python
import math

import jax
import jax.numpy as jnp
from jax import lax
from jax.experimental import pallas as pl
from jax.experimental.pallas import tpu as pltpu
from jax.sharding import PartitionSpec as P

tanh_scale = 0.7978845608028654
cubic_term = 0.044715

MESH = pl.DeviceIdType.MESH
F32 = jnp.float32
BF16 = jnp.bfloat16

NE, NZ, NX = 8, 8, 4
CAP = 72
FD = 96
SLAB = NX * FD
HID = 512
CA, CB, CT = 256, 256, 128
NC = CA + CB + CT
HALF = SLAB // 2


def gelu_pair(pre_act):
    inner_arg = tanh_scale * (pre_act + cubic_term * pre_act * pre_act * pre_act)
    tanh_part = jnp.tanh(inner_arg)
    activation = 0.5 * pre_act * (1.0 + tanh_part)
    derivative = 0.5 * (1.0 + tanh_part) + 0.5 * pre_act * (
        1.0 - tanh_part * tanh_part
    ) * tanh_scale * (1.0 + 3.0 * cubic_term * pre_act * pre_act)
    return (activation, derivative)


def mm(a, b):
    return jnp.dot(a, b, preferred_element_type=F32)


def mm_nt(a, b):
    return lax.dot_general(a, b, (((1,), (1,)), ((), ())), preferred_element_type=F32)


def iota(shape, dim):
    return lax.broadcasted_iota(jnp.int32, shape, dim)


def kernel(
    tok_hbm, ids_hbm, wts_hbm, gs_hbm, us_hbm, gw_hbm, uw_hbm, dw_hbm, out_ref,
    tok_ref, ids_ref, wts_ref, gs, us, gw, uw, dw, act_t, dup_t,
    onehot, pos_ref, weight_ref, snd1, rcv1, snd2, rcv2,
    xa, xb, xt, xtu, h, gg, ug,
    part, sa, sb, st, ra_p, ra_m, rax, sax, rbx, rtx, qb, qt, rbz_p, rbz_m, rtz_p, rtz_m,
    size_ref, sent, ld, a1r, a2r, axr, azpr, azmr, bzpr, bzmr, bxr, rzpr, rzmr, rxr, qzpr, qzmr, qxr,
):
    e = lax.axis_index("expert")
    z = lax.axis_index("row")
    x = lax.axis_index("col")

    def dev(de=0, dz=0, dx=0):
        return (
            lax.rem(e + (de + NE), NE),
            lax.rem(z + (dz + NZ), NZ),
            lax.rem(x + (dx + NX), NX),
        )

    def zrel(d):
        return lax.rem(z + (d + NZ), NZ)

    def xrel(d):
        return lax.rem(x + (d + NX), NX)

    def xrows(xx, size):
        return pl.ds(pl.multiple_of(xx * size, size), size)

    sent_bytes = [0, 0, 0, 0]

    def send(phase, src, dst, rs, to):
        copy = pltpu.make_async_remote_copy(
            src_ref=src, dst_ref=dst, send_sem=sent.at[phase], recv_sem=rs, device_id=to, device_id_type=MESH
        )
        copy.start()
        sent_bytes[phase] += 2 * math.prod(src.shape)
        return copy

    def wait_bytes(sem, size):
        whole = size_ref.at[pl.ds(0, size // 512)]
        pltpu.make_async_copy(whole, whole, sem).wait()

    def got(sem):
        wait_bytes(sem, 2 * FD * (CB + CT // 2))

    bar = pltpu.get_barrier_semaphore()
    partners = [dev(dz=1), dev(dz=-1)] + [dev(dx=r) for r in range(1, NX)]
    partners += [dev(de=r) for r in range(1, NE)]
    for p in partners:
        pl.semaphore_signal(bar, inc=1, device_id=p, device_id_type=MESH)
    small = [
        pltpu.make_async_copy(tok_hbm, tok_ref, ld.at[5]),
        pltpu.make_async_copy(ids_hbm, ids_ref, ld.at[6]),
        pltpu.make_async_copy(wts_hbm, wts_ref, ld.at[7]),
    ]
    loads = [
        pltpu.make_async_copy(gs_hbm.at[0], gs.at[pl.ds(0, 576)], ld.at[0]),
        pltpu.make_async_copy(us_hbm.at[0], us.at[pl.ds(0, 576)], ld.at[1]),
        pltpu.make_async_copy(dw_hbm.at[0], dw, ld.at[2]),
        pltpu.make_async_copy(gw_hbm.at[0], gw, ld.at[3]),
        pltpu.make_async_copy(uw_hbm.at[0], uw, ld.at[4]),
    ]
    for c in small + loads:
        c.start()
    for c in small:
        c.wait()

    tok_t = tok_ref[...].astype(F32).T
    ids = ids_ref[...]
    wts = wts_ref[...]
    e_iota = iota((NE, 192), 0)
    first = ids[0:1, :] == e_iota
    second = ids[1:2, :] == e_iota
    named = jnp.where(first, 1.0, jnp.where(second, 1.0, 0.0))
    weight = jnp.where(first, wts[0:1, :], jnp.where(second, wts[1:2, :], 0.0))
    earlier = jnp.where(iota((192, 192), 0) < iota((192, 192), 1), 1.0, 0.0).astype(BF16)
    pos = mm(named.astype(BF16), earlier)
    pos_ref[...] = jnp.where(named > 0.5, pos, -1.0)
    weight_ref[...] = weight
    j_iota = iota((128, 192), 0).astype(F32)
    lane = iota((FD, 128), 1)
    far_first = (4, 3, 5, 2, 6, 1, 7)

    def dispatch(i):
        oh = jnp.where(pos_ref[pl.ds(i, 1), :] == j_iota, 1.0, 0.0).astype(BF16)
        onehot[i] = oh
        scaled = (tok_t * weight_ref[pl.ds(i, 1), :]).astype(BF16)
        return mm_nt(scaled, oh).astype(BF16)

    pl.semaphore_wait(bar, len(partners))

    a2a = {}
    for r in far_first:
        to = lax.rem(e + r, NE)
        snd1[to] = dispatch(to)
        a2a[r] = send(0, snd1.at[to], rcv1.at[e], a1r.at[r], dev(de=r))
    rcv1[e] = dispatch(e)
    gs[576:640, :] = jnp.zeros((64, HID), BF16)
    us[576:640, :] = jnp.zeros((64, HID), BF16)
    h[...] = jnp.zeros_like(h)
    for r in far_first:
        a2a[r].wait_recv()
    tiles = [jnp.zeros((FD, 128), F32) for _ in range(NC // 128)]
    for s in range(NE):
        q, shift = divmod(CAP * s, 128)
        block = rcv1[s].astype(F32)
        if shift:
            block = pltpu.roll(block, shift, 1)
        if shift + CAP <= 128:
            tiles[q] += block
        else:
            tiles[q] += jnp.where(lane >= shift, block, 0.0)
            tiles[q + 1] += jnp.where(lane < shift, block, 0.0)
    tiles = [t.astype(BF16) for t in tiles]
    xb[z, xrows(x, FD), :128] = tiles[2]
    xb[z, xrows(x, FD), 128:] = tiles[3]
    tail = tiles[4].astype(F32)
    xt[z, xrows(x, FD // 2), :] = (tail[: FD // 2] + pltpu.roll(tail[FD // 2 :], 64, 1)).astype(BF16)
    xa[z, xrows(x, FD), :128] = tiles[0]
    xa[z, xrows(x, FD), 128:] = tiles[1]

    def gelu_block(b):
        def body(c, carry):
            cols = pl.ds(pl.multiple_of(c * 128, 128), 128)
            act, der = gelu_pair(gs[128 * b : 128 * b + 128, cols].astype(F32))
            der = der * us[128 * b : 128 * b + 128, cols].astype(F32)
            act_t[cols, 128 * b : 128 * b + 128] = act.T
            dup_t[cols, 128 * b : 128 * b + 128] = der.T
            return carry

        lax.fori_loop(0, HID // 128, body, 0)

    def both(k, body):
        if k in (0, 4):
            body(zrel(k))
        else:
            def step(i, carry):
                body(lax.rem(z + NZ + k - 2 * k * i, NZ))
                return carry

            lax.fori_loop(0, 2, step, 0)

    def mm_a(zz):
        cols = pl.ds(pl.multiple_of(zz * SLAB, SLAB), SLAB)
        h[:, :CA] += mm(dw[:, cols], xa[zz])

    def mm_b(zz):
        cols = pl.ds(pl.multiple_of(zz * SLAB, SLAB), SLAB)
        low = iota((FD // 2, 128), 1) < 64
        for i in range(NX):
            t = xt[zz, i * (FD // 2) : (i + 1) * (FD // 2), :].astype(F32)
            xtu[zz, FD * i : FD * i + FD // 2, :] = jnp.where(low, t, 0.0).astype(BF16)
            xtu[zz, FD * i + FD // 2 : FD * i + FD, :] = jnp.where(
                low, pltpu.roll(t, 64, 1), 0.0
            ).astype(BF16)
        h[:, CA : CA + CB] += mm(dw[:, cols], xb[zz])
        h[:, CA + CB :] += mm(dw[:, cols], xtu[zz])

    def bz(zz, to_plus, k):
        rs, to = (bzpr, dev(dz=1)) if to_plus else (bzmr, dev(dz=-1))
        for buf, size in ((xb, FD), (xt, FD // 2)):
            m = buf.at[zz, xrows(x, size)]
            send(1, m, m, rs.at[k], to)
        return rs.at[k]

    def bx(d, xx, which, dx):
        sem = bxr.at[d % NZ, which]
        for buf, size in ((xb, FD), (xt, FD // 2)):
            m = buf.at[zrel(d), xrows(xx, size)]
            send(1, m, m, sem, dev(dx=dx))
        return sem

    bzp, bzm, bxc, azp, azm = {}, {}, {}, {}, {}

    def bx_first(d):
        bxc[d, 0] = bx(d, x, 0, 1)
        bxc[d, 1] = bx(d, x, 1, -1)
        if d == 4:
            bxc[d, 2] = bx(d, x, 2, 2)

    def bx_second(d):
        if d == 4:
            return
        if d % 2 == 0:
            got(bxc[d, 0])
            bxc[d, 2] = bx(d, xrel(-1), 2, 1)
        else:
            got(bxc[d, 1])
            bxc[d, 2] = bx(d, xrel(1), 2, -1)

    def bx_done(d):
        if d == 4:
            got(bxc[d, 0])
        got(bxc[d, 1 if d % 2 == 0 else 0])
        got(bxc[d, 2])

    def az(zz, j, to_plus, k):
        rs, to = (azpr, dev(dz=1)) if to_plus else (azmr, dev(dz=-1))
        m = xa.at[zz, xrows(xrel(j), FD)]
        return send(1, m, m, rs.at[k, j], to)

    def ds(k):
        return (k,) if k in (0, 4) else (-k, k)

    order = (0, 1, 3, 2)
    plus_last, minus_last = order[:2], order[2:]

    bzp[0] = bz(z, True, 0)
    bzm[0] = bz(z, False, 0)
    azp[0, 0] = az(z, 0, True, 0)
    azm[0, 0] = az(z, 0, False, 0)
    own = xa.at[z, xrows(x, FD)]
    ax = {r: send(1, own, own, axr.at[r], dev(dx=r)) for r in (1, 3, 2)}
    bx_first(0)
    for c in loads[:2]:
        c.wait()

    def b_step(k):
        got(bzp[k - 1])
        if k <= 3:
            bzp[k] = bz(zrel(-k), True, k)
            got(bzm[k - 1])
            if k <= 2:
                bzm[k] = bz(zrel(k), False, k)
        for d in ds(k):
            bx_first(d)

    def a_step(k, i):
        jp, jm = order[i], order[i]
        if k == 4:
            jm = order[i + 2]
        azp[k - 1, jp].wait_recv()
        if k <= 2 or (k == 3 and jp in plus_last):
            azp[k, jp] = az(zrel(-k), jp, True, k)
        azm[k - 1, jm].wait_recv()
        if k <= 2 or (k == 3 and jm in minus_last):
            azm[k, jm] = az(zrel(k), jm, False, k)

    def second(k):
        for d in ds(k):
            bx_second(d)

    def done(k):
        for d in ds(k):
            bx_done(d)
        both(k, mm_b)

    for j in order[1:]:
        ax[NX - j].wait_recv()
        azp[0, j] = az(z, j, True, 0)
        azm[0, j] = az(z, j, False, 0)
    b_step(1)
    second(0)
    a_step(1, 0)
    b_step(2)
    loads[2].wait()
    both(0, mm_a)
    a_step(1, 1)
    gelu_block(0)
    a_step(1, 2)
    second(1)
    b_step(3)
    a_step(1, 3)
    gelu_block(1)
    both(1, mm_a)
    a_step(2, 0)
    done(0)
    a_step(2, 1)
    second(2)
    a_step(2, 2)
    b_step(4)
    gelu_block(2)
    a_step(2, 3)
    done(1)
    a_step(3, 0)
    both(2, mm_a)
    second(3)
    a_step(3, 1)
    gelu_block(3)
    a_step(3, 2)
    a_step(3, 3)
    done(2)
    gelu_block(4)
    both(3, mm_a)
    a_step(4, 0)
    done(3)
    a_step(4, 1)
    both(4, mm_a)
    done(4)

    def hidden(cols):
        hh = h[:, cols]
        gg[:, cols] = (hh * dup_t[:, cols]).astype(BF16)
        ug[:, cols] = (hh * act_t[:, cols]).astype(BF16)

    hidden(slice(0, CA))
    for c in loads[3:]:
        c.wait()

    def mm_pa(zz):
        r = pl.ds(pl.multiple_of(zz * SLAB, SLAB), SLAB)
        part[zz, :, :CA] = mm(gw[r, :], gg[:, :CA]) + mm(uw[r, :], ug[:, :CA])

    def mm_pb(zz):
        r = pl.ds(pl.multiple_of(zz * SLAB, SLAB), SLAB)
        p = mm(gw[r, :], gg[:, CA : CA + CB]) + mm(uw[r, :], ug[:, CA : CA + CB])
        part[zz, :, CA : CA + CB] = p
        sb[zz] = p.astype(BF16)
        t = mm(gw[r, :], gg[:, CA + CB :]) + mm(uw[r, :], ug[:, CA + CB :])
        part[zz, :, CA + CB :] = t
        for i in range(NX):
            st[zz, i * (FD // 2) : (i + 1) * (FD // 2), :] = (
                t[FD * i : FD * i + FD // 2] + pltpu.roll(t[FD * i + FD // 2 : FD * i + FD], 64, 1)
            ).astype(BF16)

    rap, ram = {}, {}

    def ra(k, j, to_plus):
        zz = zrel(4 - k) if to_plus else zrel(k - 4)
        rs, to, rb, kept = (rzpr, dev(dz=1), ra_p, rap) if to_plus else (rzmr, dev(dz=-1), ra_m, ram)
        r = xrows(xrel(j), FD)
        v = part[zz, r, :CA]
        if (k - 1, j) in kept:
            kept[k - 1, j].wait_recv()
            v = v + rb[k - 1, r].astype(F32)
        sa[zz, r] = v.astype(BF16)
        kept[k, j] = send(2, sa.at[zz, r], rb.at[k, r], rs.at[k, j], to)

    def rx(d, xx, which, dx):
        i = d % NZ
        zz = zrel(d)
        sem = rxr.at[i, which]
        send(2, sb.at[zz, xrows(xx, FD)], rbx.at[i, which], sem, dev(dx=dx))
        send(2, st.at[zz, xrows(xx, FD // 2)], rtx.at[i, which], sem, dev(dx=dx))
        return sem

    rxc = {}

    def rx_first(d):
        s = 1 if d % 2 == 0 else -1
        rxc[d, 0] = rx(d, xrel(2), 0, 2 if d == 0 else s)
        rxc[d, 1] = rx(d, xrel(-s), 1, -s)
        if d == 0:
            rxc[d, 2] = rx(d, xrel(s), 2, s)

    def tail_of(zz, xx):
        base = pl.multiple_of(xx * FD, FD // 2)
        top = part[zz, pl.ds(base, FD // 2), CA + CB :]
        bot = part[zz, pl.ds(pl.multiple_of(base + FD // 2, FD // 2), FD // 2), CA + CB :]
        return top + pltpu.roll(bot, 64, 1)

    def rx_second(d):
        if d == 0:
            return
        s = 1 if d % 2 == 0 else -1
        i = d % NZ
        zz = zrel(d)
        xx = xrel(s)
        got(rxc[d, 0])
        sb[zz, xrows(xx, FD), :] = (
            part[zz, xrows(xx, FD), CA : CA + CB] + rbx[i, 0].astype(F32)
        ).astype(BF16)
        st[zz, xrows(xx, FD // 2), :] = (tail_of(zz, xx) + rtx[i, 0].astype(F32)).astype(BF16)
        rxc[d, 2] = rx(d, xx, 2, s)

    def rx_done(d):
        i = d % NZ
        zz = zrel(d)
        got(rxc[d, 1])
        got(rxc[d, 2])
        m = part[zz, xrows(x, FD), CA : CA + CB] + rbx[i, 1].astype(F32) + rbx[i, 2].astype(F32)
        t = tail_of(zz, x) + rtx[i, 1].astype(F32) + rtx[i, 2].astype(F32)
        if d == 0:
            got(rxc[d, 0])
            m = m + rbx[i, 0].astype(F32)
            t = t + rtx[i, 0].astype(F32)
        return m, t

    qc = {}

    def q_send(k, to_plus, m, t):
        i = (4 - k) % NZ if to_plus else (k - 4) % NZ
        qb[i] = m.astype(BF16)
        qt[i] = t.astype(BF16)
        rs, to, rb, rt = (
            (qzpr, dev(dz=1), rbz_p, rtz_p) if to_plus else (qzmr, dev(dz=-1), rbz_m, rtz_m)
        )
        send(2, qb.at[i], rb.at[k], rs.at[k], to)
        send(2, qt.at[i], rt.at[k], rs.at[k], to)
        qc[k, to_plus] = rs.at[k]

    def q_stage(k):
        if k == 0:
            m, t = rx_done(4)
            q_send(0, True, m, t)
            return
        m, t = rx_done(4 - k)
        got(qc[k - 1, True])
        q_send(k, True, m + rbz_p[k - 1].astype(F32), t + rtz_p[k - 1].astype(F32))
        m, t = rx_done(k - 4)
        if k >= 2:
            got(qc[k - 1, False])
            m = m + rbz_m[k - 1].astype(F32)
            t = t + rtz_m[k - 1].astype(F32)
        q_send(k, False, m, t)

    orders_p = ((2, 0), (3, 1, 2, 0), (3, 2, 1, 0), (2, 3, 1, 0))
    orders_m = ((3, 1), (2, 0, 3, 1), (2, 3, 0, 1), (2, 3, 1, 0))

    def ra_both(k, i):
        ra(k, orders_p[k][i], True)
        ra(k, orders_m[k][i], False)

    def firsts(k):
        both(k, mm_pb)
        for d in ds(k):
            rx_first(d)

    def seconds(k):
        for d in ds(k):
            rx_second(d)

    sx = []
    own_a = []

    def final_a(j):
        rap[3, j].wait_recv()
        ram[3, j].wait_recv()
        r = xrows(xrel(j), FD)
        v = part[z, r, :CA] + ra_p[3, r].astype(F32) + ra_m[3, r].astype(F32)
        if j:
            sax[r, :] = v.astype(BF16)
            sx.append(send(2, sax.at[r], rax.at[j], qxr.at[j], dev(dx=j)))
        else:
            own_a.append(v)

    both(4, mm_pa)
    ra_both(0, 0)
    ra_both(0, 1)
    hidden(slice(CA, NC))
    firsts(4)
    both(3, mm_pa)
    ra_both(1, 0)
    ra_both(1, 1)
    firsts(3)
    ra_both(1, 2)
    ra_both(1, 3)
    seconds(4)
    both(2, mm_pa)
    firsts(2)
    ra_both(2, 0)
    ra_both(2, 1)
    seconds(3)
    q_stage(0)
    ra_both(2, 2)
    firsts(1)
    ra_both(2, 3)
    both(1, mm_pa)
    seconds(2)
    q_stage(1)
    ra_both(3, 0)
    firsts(0)
    ra_both(3, 1)
    seconds(1)
    q_stage(2)
    ra_both(3, 2)
    ra_both(3, 3)
    both(0, mm_pa)
    final_a(2)
    q_stage(3)
    final_a(3)
    final_a(1)
    final_a(0)
    m, t = rx_done(0)
    got(qc[3, True])
    got(qc[3, False])
    m = m + rbz_p[3].astype(F32) + rbz_m[3].astype(F32)
    t = t + rtz_p[3].astype(F32) + rtz_m[3].astype(F32)
    low = iota((FD // 2, 128), 1) < 64
    t = jnp.concatenate([jnp.where(low, t, 0.0), jnp.where(low, pltpu.roll(t, 64, 1), 0.0)], axis=0)
    a = own_a[0]
    for c in sx:
        c.wait_recv()
    for r in range(1, NX):
        a = a + rax[r].astype(F32)

    tiles = [v.astype(BF16).astype(F32) for v in (a[:, :128], a[:, 128:], m[:, :128], m[:, 128:], t)]
    for s in range(NE):
        q, shift = divmod(CAP * s, 128)
        block = tiles[q]
        if shift + CAP > 128:
            block = jnp.where(lane >= shift, block, tiles[q + 1])
        if shift:
            block = pltpu.roll(block, 128 - shift, 1)
        snd2[s] = block.astype(BF16)
    back = {}
    for r in far_first:
        to = lax.rem(e + r, NE)
        back[r] = send(3, snd2.at[to], rcv2.at[e], a2r.at[r], dev(de=r))
    o = mm(snd2[e], onehot[e])
    for r in (1, 7, 2, 6, 3, 5, 4):
        back[r].wait_recv()
        i = lax.rem(e + NE - r, NE)
        o += mm(rcv2[i], onehot[i])
    out_ref[...] = o.T.astype(BF16)
    for phase, size in enumerate(sent_bytes):
        wait_bytes(sent.at[phase], size)


def per_device(tokens_grad, expert_ids, combine_weights, gate_saved, up_saved, gate_weight, up_weight, down_weight):
    vmem = pl.BlockSpec(memory_space=pltpu.VMEM)
    hbm = pl.BlockSpec(memory_space=pl.ANY)
    dma = pltpu.SemaphoreType.DMA
    v = pltpu.VMEM
    scratch = [
        v((192, FD), BF16), v((2, 192), jnp.int32), v((2, 192), F32),
        v((640, HID), BF16), v((640, HID), BF16),
        v((3072, HID), BF16), v((3072, HID), BF16), v((HID, 3072), BF16),
        v((HID, NC), F32), v((HID, NC), F32),
        v((NE, 128, 192), BF16), v((NE, 192), F32), v((NE, 192), F32),
        v((NE, FD, 128), BF16), v((NE, FD, 128), BF16), v((NE, FD, 128), BF16), v((NE, FD, 128), BF16),
        v((NZ, SLAB, CA), BF16), v((NZ, SLAB, CB), BF16), v((NZ, HALF, CT), BF16), v((NZ, SLAB, CT), BF16),
        v((HID, NC), F32), v((HID, NC), BF16), v((HID, NC), BF16),
        v((NZ, SLAB, NC), F32),
        v((NZ, SLAB, CA), BF16), v((NZ, SLAB, CB), BF16), v((NZ, HALF, CT), BF16),
        v((4, SLAB, CA), BF16), v((4, SLAB, CA), BF16),
        v((NX, FD, CA), BF16), v((SLAB, CA), BF16),
        v((NZ, 3, FD, CB), BF16), v((NZ, 3, FD // 2, CT), BF16),
        v((NZ, FD, CB), BF16), v((NZ, FD // 2, CT), BF16),
        v((4, FD, CB), BF16), v((4, FD, CB), BF16), v((4, FD // 2, CT), BF16), v((4, FD // 2, CT), BF16),
        v((6720, 128), F32),
        dma((4,)), dma((8,)), dma((NE,)), dma((NE,)),
        dma((NX,)), dma((4, NX)), dma((4, NX)), dma((4,)), dma((3,)), dma((NZ, 3)),
        dma((4, NX)), dma((4, NX)), dma((NZ, 3)), dma((4,)), dma((4,)), dma((NX,)),
    ]
    return pl.pallas_call(
        kernel,
        out_shape=pltpu.VMEM(tokens_grad.shape, BF16),
        in_specs=[hbm] * 8,
        out_specs=vmem,
        scratch_shapes=scratch,
        compiler_params=pltpu.CompilerParams(
            collective_id=0, has_side_effects=True, vmem_limit_bytes=60 * 2**20
        ),
        name="moe_backward",
    )(tokens_grad, expert_ids.T, combine_weights.T, gate_saved, up_saved, gate_weight, up_weight, down_weight)


def solution(mesh):
    in_specs = (
        P("expert", ("row", "col")),
        P("expert", None),
        P("expert", None),
        P("expert", None, ("row", "col")),
        P("expert", None, ("row", "col")),
        P("expert", None, ("row", "col")),
        P("expert", None, ("row", "col")),
        P("expert", ("row", "col"), None),
    )
    out_specs = P("expert", ("row", "col"))
    return jax.shard_map(
        per_device, mesh=mesh, in_specs=in_specs, out_specs=out_specs, check_vma=False
    )
```

```python
import math

import jax
import jax.numpy as jnp
from jax import lax
from jax.experimental import pallas as pl
from jax.experimental.pallas import tpu as pltpu
from jax.sharding import PartitionSpec as P

tanh_scale = 0.7978845608028654
cubic_term = 0.044715

MESH = pl.DeviceIdType.MESH
F32 = jnp.float32
BF16 = jnp.bfloat16

NE, NZ, NX = 8, 8, 4
CAP = 72
FD = 96
SLAB = NX * FD
HID = 512
CA, CB, CT = 256, 256, 128
NC = CA + CB + CT
HALF = SLAB // 2


def gelu_pair(pre_act):
    inner_arg = tanh_scale * (pre_act + cubic_term * pre_act * pre_act * pre_act)
    tanh_part = jnp.tanh(inner_arg)
    activation = 0.5 * pre_act * (1.0 + tanh_part)
    derivative = 0.5 * (1.0 + tanh_part) + 0.5 * pre_act * (
        1.0 - tanh_part * tanh_part
    ) * tanh_scale * (1.0 + 3.0 * cubic_term * pre_act * pre_act)
    return (activation, derivative)


def mm(a, b):
    return jnp.dot(a, b, preferred_element_type=F32)


def mm_nt(a, b):
    return lax.dot_general(a, b, (((1,), (1,)), ((), ())), preferred_element_type=F32)


def iota(shape, dim):
    return lax.broadcasted_iota(jnp.int32, shape, dim)


def pack(block):
    half, rows = FD // 2, 16
    lane = iota((half, 128), 1)
    top = jnp.where(lane < 64, block[:half], pltpu.roll(block[half:], 64, 1))
    lane = iota((rows, 128), 1)
    rest = jnp.zeros((rows, 128), F32)
    for g in range(FD // rows):
        moved = pltpu.roll(block[rows * g : rows * g + rows], (64 + 8 * g) % 128, 1)
        rest += jnp.where((lane >= 8 * g) & (lane < 8 * g + 8), moved, 0.0)
    return jnp.concatenate([top, rest], axis=0).astype(BF16)


def unpack(packed):
    half, rows = FD // 2, 16
    packed = packed.astype(F32)
    lane = iota((rows, 128), 1)
    top, rest = packed[:half], packed[half:]
    both = jnp.concatenate([top, pltpu.roll(top, 64, 1)], axis=0)
    moved = jnp.concatenate(
        [pltpu.roll(rest, (64 - 8 * g) % 128, 1) for g in range(FD // rows)], axis=0
    )
    lane = iota((FD, 128), 1)
    return jnp.where(lane < 64, both, jnp.where(lane < CAP, moved, 0.0))


def kernel(
    tok_hbm, ids_hbm, wts_hbm, gs_hbm, us_hbm, gw_hbm, uw_hbm, dw_hbm, out_ref,
    tok_ref, ids_ref, wts_ref, gs, us, gw, uw, dw, act_t, dup_t,
    onehot, pos_ref, weight_ref, snd1, rcv1, snd2, rcv2,
    xa, xb, xt, xtu, h, gg, ug,
    part, sa, sb, st, ra_p, ra_m, rax, sax, rbx, rtx, qb, qt, rbz_p, rbz_m, rtz_p, rtz_m,
    size_ref, sent, ld, a1r, a2r, axr, azpr, azmr, bzpr, bzmr, bxr, rzpr, rzmr, rxr, qzpr, qzmr, qxr,
):
    e = lax.axis_index("expert")
    z = lax.axis_index("row")
    x = lax.axis_index("col")

    def dev(de=0, dz=0, dx=0):
        return (
            lax.rem(e + (de + NE), NE),
            lax.rem(z + (dz + NZ), NZ),
            lax.rem(x + (dx + NX), NX),
        )

    def zrel(d):
        return lax.rem(z + (d + NZ), NZ)

    def xrel(d):
        return lax.rem(x + (d + NX), NX)

    def xrows(xx, size):
        return pl.ds(pl.multiple_of(xx * size, size), size)

    sent_bytes = [0, 0, 0, 0]

    def send(phase, src, dst, rs, to):
        copy = pltpu.make_async_remote_copy(
            src_ref=src, dst_ref=dst, send_sem=sent.at[phase], recv_sem=rs, device_id=to, device_id_type=MESH
        )
        copy.start()
        sent_bytes[phase] += 2 * math.prod(src.shape)
        return copy

    def wait_bytes(sem, size):
        whole = size_ref.at[pl.ds(0, size // 512)]
        pltpu.make_async_copy(whole, whole, sem).wait()

    def got(sem):
        wait_bytes(sem, 2 * FD * (CB + CT // 2))

    bar = pltpu.get_barrier_semaphore()
    partners = [dev(dz=1), dev(dz=-1)] + [dev(dx=r) for r in range(1, NX)]
    partners += [dev(de=r) for r in range(1, NE)]
    for p in partners:
        pl.semaphore_signal(bar, inc=1, device_id=p, device_id_type=MESH)
    small = [
        pltpu.make_async_copy(tok_hbm, tok_ref, ld.at[5]),
        pltpu.make_async_copy(ids_hbm, ids_ref, ld.at[6]),
        pltpu.make_async_copy(wts_hbm, wts_ref, ld.at[7]),
    ]
    loads = [
        pltpu.make_async_copy(gs_hbm.at[0], gs.at[pl.ds(0, 576)], ld.at[0]),
        pltpu.make_async_copy(us_hbm.at[0], us.at[pl.ds(0, 576)], ld.at[1]),
        pltpu.make_async_copy(dw_hbm.at[0], dw, ld.at[2]),
        pltpu.make_async_copy(gw_hbm.at[0], gw, ld.at[3]),
        pltpu.make_async_copy(uw_hbm.at[0], uw, ld.at[4]),
    ]
    for c in small + loads:
        c.start()
    for c in small:
        c.wait()

    tok_t = tok_ref[...].astype(F32).T
    ids = ids_ref[...]
    wts = wts_ref[...]
    e_iota = iota((NE, 192), 0)
    first = ids[0:1, :] == e_iota
    second = ids[1:2, :] == e_iota
    named = jnp.where(first, 1.0, jnp.where(second, 1.0, 0.0))
    weight = jnp.where(first, wts[0:1, :], jnp.where(second, wts[1:2, :], 0.0))
    earlier = jnp.where(iota((192, 192), 0) < iota((192, 192), 1), 1.0, 0.0).astype(BF16)
    pos = mm(named.astype(BF16), earlier)
    pos_ref[...] = jnp.where(named > 0.5, pos, -1.0)
    weight_ref[...] = weight
    j_iota = iota((128, 192), 0).astype(F32)
    lane = iota((FD, 128), 1)
    far_first = (4, 3, 5, 2, 6, 1, 7)

    def dispatch(i):
        oh = jnp.where(pos_ref[pl.ds(i, 1), :] == j_iota, 1.0, 0.0).astype(BF16)
        onehot[i] = oh
        scaled = (tok_t * weight_ref[pl.ds(i, 1), :]).astype(BF16)
        return pack(mm_nt(scaled, oh))

    blocks = [dispatch(i) for i in range(NE)]
    for i in range(NE):
        snd1[i] = blocks[i]
    pl.semaphore_wait(bar, len(partners))

    for r in far_first:
        to = lax.rem(e + r, NE)
        send(0, snd1.at[to], rcv1.at[e], a1r.at[0], dev(de=r))
    rcv1[e] = snd1[e]
    gs[576:640, :] = jnp.zeros((64, HID), BF16)
    us[576:640, :] = jnp.zeros((64, HID), BF16)
    h[...] = jnp.zeros_like(h)
    wait_bytes(a1r.at[0], (NE - 1) * 64 * 128 * 2)
    tiles = [jnp.zeros((FD, 128), F32) for _ in range(NC // 128)]
    for s in range(NE):
        q, shift = divmod(CAP * s, 128)
        block = unpack(rcv1[s])
        if shift:
            block = pltpu.roll(block, shift, 1)
        if shift + CAP <= 128:
            tiles[q] += block
        else:
            tiles[q] += jnp.where(lane >= shift, block, 0.0)
            tiles[q + 1] += jnp.where(lane < shift, block, 0.0)
    tiles = [t.astype(BF16) for t in tiles]
    xb[z, xrows(x, FD), :128] = tiles[2]
    xb[z, xrows(x, FD), 128:] = tiles[3]
    tail = tiles[4].astype(F32)
    xt[z, xrows(x, FD // 2), :] = (tail[: FD // 2] + pltpu.roll(tail[FD // 2 :], 64, 1)).astype(BF16)
    xa[z, xrows(x, FD), :128] = tiles[0]
    xa[z, xrows(x, FD), 128:] = tiles[1]

    def gelu_block(b):
        def body(c, carry):
            cols = pl.ds(pl.multiple_of(c * 128, 128), 128)
            act, der = gelu_pair(gs[128 * b : 128 * b + 128, cols].astype(F32))
            der = der * us[128 * b : 128 * b + 128, cols].astype(F32)
            act_t[cols, 128 * b : 128 * b + 128] = act.T
            dup_t[cols, 128 * b : 128 * b + 128] = der.T
            return carry

        lax.fori_loop(0, HID // 128, body, 0)

    def both(k, body):
        if k in (0, 4):
            body(zrel(k))
        else:
            def step(i, carry):
                body(lax.rem(z + NZ + k - 2 * k * i, NZ))
                return carry

            lax.fori_loop(0, 2, step, 0)

    def mm_a(zz):
        cols = pl.ds(pl.multiple_of(zz * SLAB, SLAB), SLAB)
        h[:, :CA] += mm(dw[:, cols], xa[zz])

    def mm_b(zz):
        cols = pl.ds(pl.multiple_of(zz * SLAB, SLAB), SLAB)
        low = iota((FD // 2, 128), 1) < 64
        for i in range(NX):
            t = xt[zz, i * (FD // 2) : (i + 1) * (FD // 2), :].astype(F32)
            xtu[zz, FD * i : FD * i + FD // 2, :] = jnp.where(low, t, 0.0).astype(BF16)
            xtu[zz, FD * i + FD // 2 : FD * i + FD, :] = jnp.where(
                low, pltpu.roll(t, 64, 1), 0.0
            ).astype(BF16)
        h[:, CA : CA + CB] += mm(dw[:, cols], xb[zz])
        h[:, CA + CB :] += mm(dw[:, cols], xtu[zz])

    def bz(zz, to_plus, k):
        rs, to = (bzpr, dev(dz=1)) if to_plus else (bzmr, dev(dz=-1))
        for buf, size in ((xb, FD), (xt, FD // 2)):
            m = buf.at[zz, xrows(x, size)]
            send(1, m, m, rs.at[k], to)
        return rs.at[k]

    def bx(d, xx, which, dx):
        sem = bxr.at[d % NZ, which]
        for buf, size in ((xb, FD), (xt, FD // 2)):
            m = buf.at[zrel(d), xrows(xx, size)]
            send(1, m, m, sem, dev(dx=dx))
        return sem

    bzp, bzm, bxc, azp, azm = {}, {}, {}, {}, {}

    def bx_first(d):
        bxc[d, 0] = bx(d, x, 0, 1)
        bxc[d, 1] = bx(d, x, 1, -1)
        if d == 4:
            bxc[d, 2] = bx(d, x, 2, 2)

    def bx_second(d):
        if d == 4:
            return
        if d % 2 == 0:
            got(bxc[d, 0])
            bxc[d, 2] = bx(d, xrel(-1), 2, 1)
        else:
            got(bxc[d, 1])
            bxc[d, 2] = bx(d, xrel(1), 2, -1)

    def bx_done(d):
        if d == 4:
            got(bxc[d, 0])
        got(bxc[d, 1 if d % 2 == 0 else 0])
        got(bxc[d, 2])

    def az(zz, j, to_plus, k):
        rs, to = (azpr, dev(dz=1)) if to_plus else (azmr, dev(dz=-1))
        m = xa.at[zz, xrows(xrel(j), FD)]
        return send(1, m, m, rs.at[k, j], to)

    def ds(k):
        return (k,) if k in (0, 4) else (-k, k)

    order = (0, 1, 3, 2)
    plus_last, minus_last = order[:2], order[2:]

    bzp[0] = bz(z, True, 0)
    bzm[0] = bz(z, False, 0)
    azp[0, 0] = az(z, 0, True, 0)
    azm[0, 0] = az(z, 0, False, 0)
    own = xa.at[z, xrows(x, FD)]
    ax = {r: send(1, own, own, axr.at[r], dev(dx=r)) for r in (1, 3, 2)}
    bx_first(0)
    for c in loads[:2]:
        c.wait()

    def b_step(k):
        got(bzp[k - 1])
        if k <= 3:
            bzp[k] = bz(zrel(-k), True, k)
            got(bzm[k - 1])
            if k <= 2:
                bzm[k] = bz(zrel(k), False, k)
        for d in ds(k):
            bx_first(d)

    def a_step(k, i):
        jp, jm = order[i], order[i]
        if k == 4:
            jm = order[i + 2]
        azp[k - 1, jp].wait_recv()
        if k <= 2 or (k == 3 and jp in plus_last):
            azp[k, jp] = az(zrel(-k), jp, True, k)
        azm[k - 1, jm].wait_recv()
        if k <= 2 or (k == 3 and jm in minus_last):
            azm[k, jm] = az(zrel(k), jm, False, k)

    def second(k):
        for d in ds(k):
            bx_second(d)

    def done(k):
        for d in ds(k):
            bx_done(d)
        both(k, mm_b)

    for j in order[1:]:
        ax[NX - j].wait_recv()
        azp[0, j] = az(z, j, True, 0)
        azm[0, j] = az(z, j, False, 0)
    b_step(1)
    second(0)
    a_step(1, 0)
    b_step(2)
    loads[2].wait()
    both(0, mm_a)
    a_step(1, 1)
    gelu_block(0)
    a_step(1, 2)
    second(1)
    b_step(3)
    a_step(1, 3)
    gelu_block(1)
    both(1, mm_a)
    a_step(2, 0)
    done(0)
    a_step(2, 1)
    second(2)
    a_step(2, 2)
    b_step(4)
    gelu_block(2)
    a_step(2, 3)
    done(1)
    a_step(3, 0)
    both(2, mm_a)
    second(3)
    a_step(3, 1)
    gelu_block(3)
    a_step(3, 2)
    a_step(3, 3)
    done(2)
    gelu_block(4)
    both(3, mm_a)
    a_step(4, 0)
    done(3)
    a_step(4, 1)
    both(4, mm_a)
    done(4)

    def hidden(cols):
        hh = h[:, cols]
        gg[:, cols] = (hh * dup_t[:, cols]).astype(BF16)
        ug[:, cols] = (hh * act_t[:, cols]).astype(BF16)

    hidden(slice(0, CA))
    for c in loads[3:]:
        c.wait()

    def mm_pa(zz):
        r = pl.ds(pl.multiple_of(zz * SLAB, SLAB), SLAB)
        part[zz, :, :CA] = mm(gw[r, :], gg[:, :CA]) + mm(uw[r, :], ug[:, :CA])

    def mm_pb(zz):
        r = pl.ds(pl.multiple_of(zz * SLAB, SLAB), SLAB)
        p = mm(gw[r, :], gg[:, CA : CA + CB]) + mm(uw[r, :], ug[:, CA : CA + CB])
        part[zz, :, CA : CA + CB] = p
        sb[zz] = p.astype(BF16)
        t = mm(gw[r, :], gg[:, CA + CB :]) + mm(uw[r, :], ug[:, CA + CB :])
        part[zz, :, CA + CB :] = t
        for i in range(NX):
            st[zz, i * (FD // 2) : (i + 1) * (FD // 2), :] = (
                t[FD * i : FD * i + FD // 2] + pltpu.roll(t[FD * i + FD // 2 : FD * i + FD], 64, 1)
            ).astype(BF16)

    rap, ram = {}, {}

    def ra(k, j, to_plus):
        zz = zrel(4 - k) if to_plus else zrel(k - 4)
        rs, to, rb, kept = (rzpr, dev(dz=1), ra_p, rap) if to_plus else (rzmr, dev(dz=-1), ra_m, ram)
        r = xrows(xrel(j), FD)
        v = part[zz, r, :CA]
        if (k - 1, j) in kept:
            kept[k - 1, j].wait_recv()
            v = v + rb[k - 1, r].astype(F32)
        sa[zz, r] = v.astype(BF16)
        kept[k, j] = send(2, sa.at[zz, r], rb.at[k, r], rs.at[k, j], to)

    def rx(d, xx, which, dx):
        i = d % NZ
        zz = zrel(d)
        sem = rxr.at[i, which]
        send(2, sb.at[zz, xrows(xx, FD)], rbx.at[i, which], sem, dev(dx=dx))
        send(2, st.at[zz, xrows(xx, FD // 2)], rtx.at[i, which], sem, dev(dx=dx))
        return sem

    rxc = {}

    def rx_first(d):
        s = 1 if d % 2 == 0 else -1
        rxc[d, 0] = rx(d, xrel(2), 0, 2 if d == 0 else s)
        rxc[d, 1] = rx(d, xrel(-s), 1, -s)
        if d == 0:
            rxc[d, 2] = rx(d, xrel(s), 2, s)

    def tail_of(zz, xx):
        base = pl.multiple_of(xx * FD, FD // 2)
        top = part[zz, pl.ds(base, FD // 2), CA + CB :]
        bot = part[zz, pl.ds(pl.multiple_of(base + FD // 2, FD // 2), FD // 2), CA + CB :]
        return top + pltpu.roll(bot, 64, 1)

    def rx_second(d):
        if d == 0:
            return
        s = 1 if d % 2 == 0 else -1
        i = d % NZ
        zz = zrel(d)
        xx = xrel(s)
        got(rxc[d, 0])
        sb[zz, xrows(xx, FD), :] = (
            part[zz, xrows(xx, FD), CA : CA + CB] + rbx[i, 0].astype(F32)
        ).astype(BF16)
        st[zz, xrows(xx, FD // 2), :] = (tail_of(zz, xx) + rtx[i, 0].astype(F32)).astype(BF16)
        rxc[d, 2] = rx(d, xx, 2, s)

    def rx_done(d):
        i = d % NZ
        zz = zrel(d)
        got(rxc[d, 1])
        got(rxc[d, 2])
        m = part[zz, xrows(x, FD), CA : CA + CB] + rbx[i, 1].astype(F32) + rbx[i, 2].astype(F32)
        t = tail_of(zz, x) + rtx[i, 1].astype(F32) + rtx[i, 2].astype(F32)
        if d == 0:
            got(rxc[d, 0])
            m = m + rbx[i, 0].astype(F32)
            t = t + rtx[i, 0].astype(F32)
        return m, t

    qc = {}

    def q_send(k, to_plus, m, t):
        i = (4 - k) % NZ if to_plus else (k - 4) % NZ
        qb[i] = m.astype(BF16)
        qt[i] = t.astype(BF16)
        rs, to, rb, rt = (
            (qzpr, dev(dz=1), rbz_p, rtz_p) if to_plus else (qzmr, dev(dz=-1), rbz_m, rtz_m)
        )
        send(2, qb.at[i], rb.at[k], rs.at[k], to)
        send(2, qt.at[i], rt.at[k], rs.at[k], to)
        qc[k, to_plus] = rs.at[k]

    def q_stage(k):
        if k == 0:
            m, t = rx_done(4)
            q_send(0, True, m, t)
            return
        m, t = rx_done(4 - k)
        got(qc[k - 1, True])
        q_send(k, True, m + rbz_p[k - 1].astype(F32), t + rtz_p[k - 1].astype(F32))
        m, t = rx_done(k - 4)
        if k >= 2:
            got(qc[k - 1, False])
            m = m + rbz_m[k - 1].astype(F32)
            t = t + rtz_m[k - 1].astype(F32)
        q_send(k, False, m, t)

    orders_p = ((2, 0), (3, 1, 2, 0), (3, 2, 1, 0), (2, 3, 1, 0))
    orders_m = ((3, 1), (2, 0, 3, 1), (2, 3, 0, 1), (2, 3, 1, 0))

    def ra_both(k, i):
        ra(k, orders_p[k][i], True)
        ra(k, orders_m[k][i], False)

    def firsts(k):
        both(k, mm_pb)
        for d in ds(k):
            rx_first(d)

    def seconds(k):
        for d in ds(k):
            rx_second(d)

    own_a = []

    def final_a(j):
        rap[3, j].wait_recv()
        ram[3, j].wait_recv()
        r = xrows(xrel(j), FD)
        v = part[z, r, :CA] + ra_p[3, r].astype(F32) + ra_m[3, r].astype(F32)
        if j:
            sax[r, :] = v.astype(BF16)
            send(2, sax.at[r], rax.at[j], qxr.at[0], dev(dx=j))
        else:
            own_a.append(v)

    both(4, mm_pa)
    ra_both(0, 0)
    ra_both(0, 1)
    hidden(slice(CA, NC))
    firsts(4)
    both(3, mm_pa)
    ra_both(1, 0)
    ra_both(1, 1)
    firsts(3)
    ra_both(1, 2)
    ra_both(1, 3)
    seconds(4)
    both(2, mm_pa)
    firsts(2)
    ra_both(2, 0)
    ra_both(2, 1)
    seconds(3)
    q_stage(0)
    ra_both(2, 2)
    firsts(1)
    ra_both(2, 3)
    both(1, mm_pa)
    seconds(2)
    q_stage(1)
    ra_both(3, 0)
    firsts(0)
    ra_both(3, 1)
    seconds(1)
    q_stage(2)
    ra_both(3, 2)
    ra_both(3, 3)
    both(0, mm_pa)
    final_a(2)
    q_stage(3)
    final_a(3)
    final_a(1)
    final_a(0)
    m, t = rx_done(0)
    got(qc[3, True])
    got(qc[3, False])
    m = m + rbz_p[3].astype(F32) + rbz_m[3].astype(F32)
    t = t + rtz_p[3].astype(F32) + rtz_m[3].astype(F32)
    low = iota((FD // 2, 128), 1) < 64
    t = jnp.concatenate([jnp.where(low, t, 0.0), jnp.where(low, pltpu.roll(t, 64, 1), 0.0)], axis=0)
    a = own_a[0]
    wait_bytes(qxr.at[0], (NX - 1) * FD * CA * 2)
    for r in range(1, NX):
        a = a + rax[r].astype(F32)

    tiles = [v.astype(BF16).astype(F32) for v in (a[:, :128], a[:, 128:], m[:, :128], m[:, 128:], t)]
    for s in range(NE):
        q, shift = divmod(CAP * s, 128)
        block = tiles[q]
        if shift + CAP > 128:
            block = jnp.where(lane >= shift, block, tiles[q + 1])
        if shift:
            block = pltpu.roll(block, 128 - shift, 1)
        snd2[s] = pack(block)
    for r in far_first:
        to = lax.rem(e + r, NE)
        send(3, snd2.at[to], rcv2.at[e], a2r.at[0], dev(de=r))
    o = mm(unpack(snd2[e]).astype(BF16), onehot[e])
    wait_bytes(a2r.at[0], (NE - 1) * 64 * 128 * 2)
    for r in (1, 7, 2, 6, 3, 5, 4):
        i = lax.rem(e + NE - r, NE)
        o += mm(unpack(rcv2[i]).astype(BF16), onehot[i])
    out_ref[...] = o.T.astype(BF16)
    for phase, size in enumerate(sent_bytes):
        wait_bytes(sent.at[phase], size)


def per_device(tokens_grad, expert_ids, combine_weights, gate_saved, up_saved, gate_weight, up_weight, down_weight):
    vmem = pl.BlockSpec(memory_space=pltpu.VMEM)
    hbm = pl.BlockSpec(memory_space=pl.ANY)
    dma = pltpu.SemaphoreType.DMA
    v = pltpu.VMEM
    scratch = [
        v((192, FD), BF16), v((2, 192), jnp.int32), v((2, 192), F32),
        v((640, HID), BF16), v((640, HID), BF16),
        v((3072, HID), BF16), v((3072, HID), BF16), v((HID, 3072), BF16),
        v((HID, NC), F32), v((HID, NC), F32),
        v((NE, 128, 192), BF16), v((NE, 192), F32), v((NE, 192), F32),
        v((NE, 64, 128), BF16), v((NE, 64, 128), BF16), v((NE, 64, 128), BF16), v((NE, 64, 128), BF16),
        v((NZ, SLAB, CA), BF16), v((NZ, SLAB, CB), BF16), v((NZ, HALF, CT), BF16), v((NZ, SLAB, CT), BF16),
        v((HID, NC), F32), v((HID, NC), BF16), v((HID, NC), BF16),
        v((NZ, SLAB, NC), F32),
        v((NZ, SLAB, CA), BF16), v((NZ, SLAB, CB), BF16), v((NZ, HALF, CT), BF16),
        v((4, SLAB, CA), BF16), v((4, SLAB, CA), BF16),
        v((NX, FD, CA), BF16), v((SLAB, CA), BF16),
        v((NZ, 3, FD, CB), BF16), v((NZ, 3, FD // 2, CT), BF16),
        v((NZ, FD, CB), BF16), v((NZ, FD // 2, CT), BF16),
        v((4, FD, CB), BF16), v((4, FD, CB), BF16), v((4, FD // 2, CT), BF16), v((4, FD // 2, CT), BF16),
        v((6720, 128), F32),
        dma((4,)), dma((8,)), dma((1,)), dma((1,)),
        dma((NX,)), dma((4, NX)), dma((4, NX)), dma((4,)), dma((3,)), dma((NZ, 3)),
        dma((4, NX)), dma((4, NX)), dma((NZ, 3)), dma((4,)), dma((4,)), dma((1,)),
    ]
    return pl.pallas_call(
        kernel,
        out_shape=pltpu.VMEM(tokens_grad.shape, BF16),
        in_specs=[hbm] * 8,
        out_specs=vmem,
        scratch_shapes=scratch,
        compiler_params=pltpu.CompilerParams(
            collective_id=0, has_side_effects=True, vmem_limit_bytes=60 * 2**20
        ),
        name="moe_backward",
    )(tokens_grad, expert_ids.T, combine_weights.T, gate_saved, up_saved, gate_weight, up_weight, down_weight)


def solution(mesh):
    in_specs = (
        P("expert", ("row", "col")),
        P("expert", None),
        P("expert", None),
        P("expert", None, ("row", "col")),
        P("expert", None, ("row", "col")),
        P("expert", None, ("row", "col")),
        P("expert", None, ("row", "col")),
        P("expert", ("row", "col"), None),
    )
    out_specs = P("expert", ("row", "col"))
    return jax.shard_map(
        per_device, mesh=mesh, in_specs=in_specs, out_specs=out_specs, check_vma=False
    )
```

```python
import math

import jax
import jax.numpy as jnp
from jax import lax
from jax.experimental import pallas as pl
from jax.experimental.pallas import tpu as pltpu
from jax.sharding import PartitionSpec as P

tanh_scale = 0.7978845608028654
cubic_term = 0.044715

MESH = pl.DeviceIdType.MESH
F32 = jnp.float32
BF16 = jnp.bfloat16

NE, NZ, NX = 8, 8, 4
CAP = 72
FD = 96
SLAB = NX * FD
HID = 512
CA, CB, CT = 256, 256, 128
NC = CA + CB + CT
HALF = SLAB // 2


def gelu_pair(pre_act):
    inner_arg = tanh_scale * (pre_act + cubic_term * pre_act * pre_act * pre_act)
    tanh_part = jnp.tanh(inner_arg)
    activation = 0.5 * pre_act * (1.0 + tanh_part)
    derivative = 0.5 * (1.0 + tanh_part) + 0.5 * pre_act * (
        1.0 - tanh_part * tanh_part
    ) * tanh_scale * (1.0 + 3.0 * cubic_term * pre_act * pre_act)
    return (activation, derivative)


def mm(a, b):
    return jnp.dot(a, b, preferred_element_type=F32)


def mm_nt(a, b):
    return lax.dot_general(a, b, (((1,), (1,)), ((), ())), preferred_element_type=F32)


def iota(shape, dim):
    return lax.broadcasted_iota(jnp.int32, shape, dim)


def pack(block):
    half, rows = FD // 2, 16
    lane = iota((half, 128), 1)
    top = jnp.where(lane < 64, block[:half], pltpu.roll(block[half:], 64, 1))
    lane = iota((rows, 128), 1)
    rest = jnp.zeros((rows, 128), F32)
    for g in range(FD // rows):
        moved = pltpu.roll(block[rows * g : rows * g + rows], (64 + 8 * g) % 128, 1)
        rest += jnp.where((lane >= 8 * g) & (lane < 8 * g + 8), moved, 0.0)
    return jnp.concatenate([top, rest], axis=0).astype(BF16)


def unpack(packed):
    half, rows = FD // 2, 16
    packed = packed.astype(F32)
    lane = iota((rows, 128), 1)
    top, rest = packed[:half], packed[half:]
    both = jnp.concatenate([top, pltpu.roll(top, 64, 1)], axis=0)
    moved = jnp.concatenate(
        [pltpu.roll(rest, (64 - 8 * g) % 128, 1) for g in range(FD // rows)], axis=0
    )
    lane = iota((FD, 128), 1)
    return jnp.where(lane < 64, both, jnp.where(lane < CAP, moved, 0.0))


def kernel(
    tok_hbm, ids_hbm, wts_hbm, gs_hbm, us_hbm, gw_hbm, uw_hbm, dw_hbm, out_ref,
    tok_ref, ids_ref, wts_ref, gs, us, gw, uw, dw, act_t, dup_t,
    onehot, pos_ref, weight_ref, snd1, rcv1, snd2, rcv2,
    xa, xb, xt, xtu, h, gg, ug,
    part, sa, sb, st, ra_p, ra_m, rax, sax, rbx, rtx, qb, qt, rbz_p, rbz_m, rtz_p, rtz_m,
    size_ref, sent, ld, a1r, a2r, axr, azpr, azmr, bzpr, bzmr, bxr, rzpr, rzmr, rxr, qzpr, qzmr, qxr,
):
    e = lax.axis_index("expert")
    z = lax.axis_index("row")
    x = lax.axis_index("col")

    def dev(de=0, dz=0, dx=0):
        return (
            lax.rem(e + (de + NE), NE),
            lax.rem(z + (dz + NZ), NZ),
            lax.rem(x + (dx + NX), NX),
        )

    def zrel(d):
        return lax.rem(z + (d + NZ), NZ)

    def xrel(d):
        return lax.rem(x + (d + NX), NX)

    def xrows(xx, size):
        return pl.ds(pl.multiple_of(xx * size, size), size)

    sent_bytes = [0, 0, 0, 0]

    def send(phase, src, dst, rs, to):
        copy = pltpu.make_async_remote_copy(
            src_ref=src, dst_ref=dst, send_sem=sent.at[phase], recv_sem=rs, device_id=to, device_id_type=MESH
        )
        copy.start()
        sent_bytes[phase] += 2 * math.prod(src.shape)
        return copy

    def wait_bytes(sem, size):
        whole = size_ref.at[pl.ds(0, size // 512)]
        pltpu.make_async_copy(whole, whole, sem).wait()

    def got(sem):
        wait_bytes(sem, 2 * FD * (CB + CT // 2))

    bar = pltpu.get_barrier_semaphore()
    partners = [dev(dz=1), dev(dz=-1)] + [dev(dx=r) for r in range(1, NX)]
    partners += [dev(de=r) for r in range(1, NE)]
    for p in partners:
        pl.semaphore_signal(bar, inc=1, device_id=p, device_id_type=MESH)
    small = [
        pltpu.make_async_copy(tok_hbm, tok_ref, ld.at[5]),
        pltpu.make_async_copy(ids_hbm, ids_ref, ld.at[6]),
        pltpu.make_async_copy(wts_hbm, wts_ref, ld.at[7]),
    ]
    loads = [
        pltpu.make_async_copy(gs_hbm.at[0], gs.at[pl.ds(0, 576)], ld.at[0]),
        pltpu.make_async_copy(us_hbm.at[0], us.at[pl.ds(0, 576)], ld.at[1]),
        pltpu.make_async_copy(dw_hbm.at[0], dw, ld.at[2]),
        pltpu.make_async_copy(gw_hbm.at[0], gw, ld.at[3]),
        pltpu.make_async_copy(uw_hbm.at[0], uw, ld.at[4]),
    ]
    for c in small + loads:
        c.start()
    for c in small:
        c.wait()

    tok_t = tok_ref[...].astype(F32).T
    ids = ids_ref[...]
    wts = wts_ref[...]
    e_iota = iota((NE, 192), 0)
    first = ids[0:1, :] == e_iota
    second = ids[1:2, :] == e_iota
    named = jnp.where(first, 1.0, jnp.where(second, 1.0, 0.0))
    weight = jnp.where(first, wts[0:1, :], jnp.where(second, wts[1:2, :], 0.0))
    earlier = jnp.where(iota((192, 192), 0) < iota((192, 192), 1), 1.0, 0.0).astype(BF16)
    pos = mm(named.astype(BF16), earlier)
    pos_ref[...] = jnp.where(named > 0.5, pos, -1.0)
    weight_ref[...] = weight
    j_iota = iota((128, 192), 0).astype(F32)
    lane = iota((FD, 128), 1)
    far_first = (4, 3, 5, 2, 6, 1, 7)

    def dispatch(i):
        oh = jnp.where(pos_ref[pl.ds(i, 1), :] == j_iota, 1.0, 0.0).astype(BF16)
        onehot[i] = oh
        scaled = (tok_t * weight_ref[pl.ds(i, 1), :]).astype(BF16)
        return pack(mm_nt(scaled, oh))

    blocks = [dispatch(i) for i in range(NE)]
    for i in range(NE):
        snd1[i] = blocks[i]
    pl.semaphore_wait(bar, len(partners))

    for r in far_first:
        to = lax.rem(e + r, NE)
        send(0, snd1.at[to], rcv1.at[e], a1r.at[0], dev(de=r))
    rcv1[e] = snd1[e]
    gs[576:640, :] = jnp.zeros((64, HID), BF16)
    us[576:640, :] = jnp.zeros((64, HID), BF16)
    h[...] = jnp.zeros_like(h)
    def gelu_block(b):
        def body(c, carry):
            cols = pl.ds(pl.multiple_of(c * 128, 128), 128)
            act, der = gelu_pair(gs[128 * b : 128 * b + 128, cols].astype(F32))
            der = der * us[128 * b : 128 * b + 128, cols].astype(F32)
            act_t[cols, 128 * b : 128 * b + 128] = act.T
            dup_t[cols, 128 * b : 128 * b + 128] = der.T
            return carry

        lax.fori_loop(0, HID // 128, body, 0)

    for c in loads[:2]:
        c.wait()
    for b in range(5):
        gelu_block(b)
    wait_bytes(a1r.at[0], (NE - 1) * 64 * 128 * 2)
    tiles = [jnp.zeros((FD, 128), F32) for _ in range(NC // 128)]
    for s in range(NE):
        q, shift = divmod(CAP * s, 128)
        block = unpack(rcv1[s])
        if shift:
            block = pltpu.roll(block, shift, 1)
        if shift + CAP <= 128:
            tiles[q] += block
        else:
            tiles[q] += jnp.where(lane >= shift, block, 0.0)
            tiles[q + 1] += jnp.where(lane < shift, block, 0.0)
    tiles = [t.astype(BF16) for t in tiles]
    xb[z, xrows(x, FD), :128] = tiles[2]
    xb[z, xrows(x, FD), 128:] = tiles[3]
    tail = tiles[4].astype(F32)
    xt[z, xrows(x, FD // 2), :] = (tail[: FD // 2] + pltpu.roll(tail[FD // 2 :], 64, 1)).astype(BF16)
    xa[z, xrows(x, FD), :128] = tiles[0]
    xa[z, xrows(x, FD), 128:] = tiles[1]

    def both(k, body):
        if k in (0, 4):
            body(zrel(k))
        else:
            def step(i, carry):
                body(lax.rem(z + NZ + k - 2 * k * i, NZ))
                return carry

            lax.fori_loop(0, 2, step, 0)

    def mm_a(zz):
        cols = pl.ds(pl.multiple_of(zz * SLAB, SLAB), SLAB)
        h[:, :CA] += mm(dw[:, cols], xa[zz])

    def mm_b(zz):
        cols = pl.ds(pl.multiple_of(zz * SLAB, SLAB), SLAB)
        low = iota((FD // 2, 128), 1) < 64
        for i in range(NX):
            t = xt[zz, i * (FD // 2) : (i + 1) * (FD // 2), :].astype(F32)
            xtu[zz, FD * i : FD * i + FD // 2, :] = jnp.where(low, t, 0.0).astype(BF16)
            xtu[zz, FD * i + FD // 2 : FD * i + FD, :] = jnp.where(
                low, pltpu.roll(t, 64, 1), 0.0
            ).astype(BF16)
        h[:, CA : CA + CB] += mm(dw[:, cols], xb[zz])
        h[:, CA + CB :] += mm(dw[:, cols], xtu[zz])

    def bz(zz, to_plus, k):
        rs, to = (bzpr, dev(dz=1)) if to_plus else (bzmr, dev(dz=-1))
        for buf, size in ((xb, FD), (xt, FD // 2)):
            m = buf.at[zz, xrows(x, size)]
            send(1, m, m, rs.at[k], to)
        return rs.at[k]

    def bx(d, xx, which, dx):
        sem = bxr.at[d % NZ, which]
        for buf, size in ((xb, FD), (xt, FD // 2)):
            m = buf.at[zrel(d), xrows(xx, size)]
            send(1, m, m, sem, dev(dx=dx))
        return sem

    bzp, bzm, bxc, azp, azm = {}, {}, {}, {}, {}

    def bx_first(d):
        bxc[d, 0] = bx(d, x, 0, 1)
        bxc[d, 1] = bx(d, x, 1, -1)
        if d == 4:
            bxc[d, 2] = bx(d, x, 2, 2)

    def bx_second(d):
        if d == 4:
            return
        if d % 2 == 0:
            got(bxc[d, 0])
            bxc[d, 2] = bx(d, xrel(-1), 2, 1)
        else:
            got(bxc[d, 1])
            bxc[d, 2] = bx(d, xrel(1), 2, -1)

    def bx_done(d):
        if d == 4:
            got(bxc[d, 0])
        got(bxc[d, 1 if d % 2 == 0 else 0])
        got(bxc[d, 2])

    def az(zz, j, to_plus, k):
        rs, to = (azpr, dev(dz=1)) if to_plus else (azmr, dev(dz=-1))
        m = xa.at[zz, xrows(xrel(j), FD)]
        return send(1, m, m, rs.at[k, j], to)

    def ds(k):
        return (k,) if k in (0, 4) else (-k, k)

    order = (0, 1, 3, 2)
    plus_last, minus_last = order[:2], order[2:]

    bzp[0] = bz(z, True, 0)
    bzm[0] = bz(z, False, 0)
    azp[0, 0] = az(z, 0, True, 0)
    azm[0, 0] = az(z, 0, False, 0)
    own = xa.at[z, xrows(x, FD)]
    ax = {r: send(1, own, own, axr.at[r], dev(dx=r)) for r in (1, 3, 2)}
    bx_first(0)

    def b_step(k):
        got(bzp[k - 1])
        if k <= 3:
            bzp[k] = bz(zrel(-k), True, k)
            got(bzm[k - 1])
            if k <= 2:
                bzm[k] = bz(zrel(k), False, k)
        for d in ds(k):
            bx_first(d)

    def a_step(k, i):
        jp, jm = order[i], order[i]
        if k == 4:
            jm = order[i + 2]
        azp[k - 1, jp].wait_recv()
        if k <= 2 or (k == 3 and jp in plus_last):
            azp[k, jp] = az(zrel(-k), jp, True, k)
        azm[k - 1, jm].wait_recv()
        if k <= 2 or (k == 3 and jm in minus_last):
            azm[k, jm] = az(zrel(k), jm, False, k)

    def second(k):
        for d in ds(k):
            bx_second(d)

    def done(k):
        for d in ds(k):
            bx_done(d)
        both(k, mm_b)

    for j in order[1:]:
        ax[NX - j].wait_recv()
        azp[0, j] = az(z, j, True, 0)
        azm[0, j] = az(z, j, False, 0)
    b_step(1)
    second(0)
    a_step(1, 0)
    b_step(2)
    loads[2].wait()
    both(0, mm_a)
    a_step(1, 1)
    a_step(1, 2)
    second(1)
    b_step(3)
    a_step(1, 3)
    both(1, mm_a)
    a_step(2, 0)
    done(0)
    a_step(2, 1)
    second(2)
    a_step(2, 2)
    b_step(4)
    a_step(2, 3)
    done(1)
    a_step(3, 0)
    both(2, mm_a)
    second(3)
    a_step(3, 1)
    a_step(3, 2)
    a_step(3, 3)
    done(2)
    both(3, mm_a)
    a_step(4, 0)
    done(3)
    a_step(4, 1)
    both(4, mm_a)
    done(4)

    def hidden(cols):
        hh = h[:, cols]
        gg[:, cols] = (hh * dup_t[:, cols]).astype(BF16)
        ug[:, cols] = (hh * act_t[:, cols]).astype(BF16)

    hidden(slice(0, CA))
    for c in loads[3:]:
        c.wait()

    def mm_pa(zz):
        r = pl.ds(pl.multiple_of(zz * SLAB, SLAB), SLAB)
        part[zz, :, :CA] = mm(gw[r, :], gg[:, :CA]) + mm(uw[r, :], ug[:, :CA])

    def mm_pb(zz):
        r = pl.ds(pl.multiple_of(zz * SLAB, SLAB), SLAB)
        p = mm(gw[r, :], gg[:, CA : CA + CB]) + mm(uw[r, :], ug[:, CA : CA + CB])
        part[zz, :, CA : CA + CB] = p
        sb[zz] = p.astype(BF16)
        t = mm(gw[r, :], gg[:, CA + CB :]) + mm(uw[r, :], ug[:, CA + CB :])
        part[zz, :, CA + CB :] = t
        for i in range(NX):
            st[zz, i * (FD // 2) : (i + 1) * (FD // 2), :] = (
                t[FD * i : FD * i + FD // 2] + pltpu.roll(t[FD * i + FD // 2 : FD * i + FD], 64, 1)
            ).astype(BF16)

    rap, ram = {}, {}

    def ra(k, j, to_plus):
        zz = zrel(4 - k) if to_plus else zrel(k - 4)
        rs, to, rb, kept = (rzpr, dev(dz=1), ra_p, rap) if to_plus else (rzmr, dev(dz=-1), ra_m, ram)
        r = xrows(xrel(j), FD)
        v = part[zz, r, :CA]
        if (k - 1, j) in kept:
            kept[k - 1, j].wait_recv()
            v = v + rb[k - 1, r].astype(F32)
        sa[zz, r] = v.astype(BF16)
        kept[k, j] = send(2, sa.at[zz, r], rb.at[k, r], rs.at[k, j], to)

    def rx(d, xx, which, dx):
        i = d % NZ
        zz = zrel(d)
        sem = rxr.at[i, which]
        send(2, sb.at[zz, xrows(xx, FD)], rbx.at[i, which], sem, dev(dx=dx))
        send(2, st.at[zz, xrows(xx, FD // 2)], rtx.at[i, which], sem, dev(dx=dx))
        return sem

    rxc = {}

    def rx_first(d):
        s = 1 if d % 2 == 0 else -1
        rxc[d, 0] = rx(d, xrel(2), 0, 2 if d == 0 else s)
        rxc[d, 1] = rx(d, xrel(-s), 1, -s)
        if d == 0:
            rxc[d, 2] = rx(d, xrel(s), 2, s)

    def tail_of(zz, xx):
        base = pl.multiple_of(xx * FD, FD // 2)
        top = part[zz, pl.ds(base, FD // 2), CA + CB :]
        bot = part[zz, pl.ds(pl.multiple_of(base + FD // 2, FD // 2), FD // 2), CA + CB :]
        return top + pltpu.roll(bot, 64, 1)

    def rx_second(d):
        if d == 0:
            return
        s = 1 if d % 2 == 0 else -1
        i = d % NZ
        zz = zrel(d)
        xx = xrel(s)
        got(rxc[d, 0])
        sb[zz, xrows(xx, FD), :] = (
            part[zz, xrows(xx, FD), CA : CA + CB] + rbx[i, 0].astype(F32)
        ).astype(BF16)
        st[zz, xrows(xx, FD // 2), :] = (tail_of(zz, xx) + rtx[i, 0].astype(F32)).astype(BF16)
        rxc[d, 2] = rx(d, xx, 2, s)

    def rx_done(d):
        i = d % NZ
        zz = zrel(d)
        got(rxc[d, 1])
        got(rxc[d, 2])
        m = part[zz, xrows(x, FD), CA : CA + CB] + rbx[i, 1].astype(F32) + rbx[i, 2].astype(F32)
        t = tail_of(zz, x) + rtx[i, 1].astype(F32) + rtx[i, 2].astype(F32)
        if d == 0:
            got(rxc[d, 0])
            m = m + rbx[i, 0].astype(F32)
            t = t + rtx[i, 0].astype(F32)
        return m, t

    qc = {}

    def q_send(k, to_plus, m, t):
        i = (4 - k) % NZ if to_plus else (k - 4) % NZ
        qb[i] = m.astype(BF16)
        qt[i] = t.astype(BF16)
        rs, to, rb, rt = (
            (qzpr, dev(dz=1), rbz_p, rtz_p) if to_plus else (qzmr, dev(dz=-1), rbz_m, rtz_m)
        )
        send(2, qb.at[i], rb.at[k], rs.at[k], to)
        send(2, qt.at[i], rt.at[k], rs.at[k], to)
        qc[k, to_plus] = rs.at[k]

    def q_stage(k):
        if k == 0:
            m, t = rx_done(4)
            q_send(0, True, m, t)
            return
        m, t = rx_done(4 - k)
        got(qc[k - 1, True])
        q_send(k, True, m + rbz_p[k - 1].astype(F32), t + rtz_p[k - 1].astype(F32))
        m, t = rx_done(k - 4)
        if k >= 2:
            got(qc[k - 1, False])
            m = m + rbz_m[k - 1].astype(F32)
            t = t + rtz_m[k - 1].astype(F32)
        q_send(k, False, m, t)

    orders_p = ((2, 0), (3, 1, 2, 0), (3, 2, 1, 0), (2, 3, 1, 0))
    orders_m = ((3, 1), (2, 0, 3, 1), (2, 3, 0, 1), (2, 3, 1, 0))

    def ra_both(k, i):
        ra(k, orders_p[k][i], True)
        ra(k, orders_m[k][i], False)

    def firsts(k):
        both(k, mm_pb)
        for d in ds(k):
            rx_first(d)

    def seconds(k):
        for d in ds(k):
            rx_second(d)

    own_a = []

    def final_a(j):
        rap[3, j].wait_recv()
        ram[3, j].wait_recv()
        r = xrows(xrel(j), FD)
        v = part[z, r, :CA] + ra_p[3, r].astype(F32) + ra_m[3, r].astype(F32)
        if j:
            sax[r, :] = v.astype(BF16)
            send(2, sax.at[r], rax.at[j], qxr.at[0], dev(dx=j))
        else:
            own_a.append(v)

    both(4, mm_pa)
    ra_both(0, 0)
    ra_both(0, 1)
    hidden(slice(CA, NC))
    firsts(4)
    both(3, mm_pa)
    ra_both(1, 0)
    ra_both(1, 1)
    firsts(3)
    ra_both(1, 2)
    ra_both(1, 3)
    seconds(4)
    both(2, mm_pa)
    firsts(2)
    ra_both(2, 0)
    ra_both(2, 1)
    seconds(3)
    q_stage(0)
    ra_both(2, 2)
    firsts(1)
    ra_both(2, 3)
    both(1, mm_pa)
    seconds(2)
    q_stage(1)
    ra_both(3, 0)
    firsts(0)
    ra_both(3, 1)
    seconds(1)
    q_stage(2)
    ra_both(3, 2)
    ra_both(3, 3)
    both(0, mm_pa)
    final_a(2)
    q_stage(3)
    final_a(3)
    final_a(1)
    final_a(0)
    m, t = rx_done(0)
    got(qc[3, True])
    got(qc[3, False])
    m = m + rbz_p[3].astype(F32) + rbz_m[3].astype(F32)
    t = t + rtz_p[3].astype(F32) + rtz_m[3].astype(F32)
    low = iota((FD // 2, 128), 1) < 64
    t = jnp.concatenate([jnp.where(low, t, 0.0), jnp.where(low, pltpu.roll(t, 64, 1), 0.0)], axis=0)
    a = own_a[0]
    wait_bytes(qxr.at[0], (NX - 1) * FD * CA * 2)
    for r in range(1, NX):
        a = a + rax[r].astype(F32)

    tiles = [v.astype(BF16).astype(F32) for v in (a[:, :128], a[:, 128:], m[:, :128], m[:, 128:], t)]
    for s in range(NE):
        q, shift = divmod(CAP * s, 128)
        block = tiles[q]
        if shift + CAP > 128:
            block = jnp.where(lane >= shift, block, tiles[q + 1])
        if shift:
            block = pltpu.roll(block, 128 - shift, 1)
        snd2[s] = pack(block)
    for r in far_first:
        to = lax.rem(e + r, NE)
        send(3, snd2.at[to], rcv2.at[e], a2r.at[0], dev(de=r))
    o = mm(unpack(snd2[e]).astype(BF16), onehot[e])
    wait_bytes(a2r.at[0], (NE - 1) * 64 * 128 * 2)
    for r in (1, 7, 2, 6, 3, 5, 4):
        i = lax.rem(e + NE - r, NE)
        o += mm(unpack(rcv2[i]).astype(BF16), onehot[i])
    out_ref[...] = o.T.astype(BF16)
    for phase, size in enumerate(sent_bytes):
        wait_bytes(sent.at[phase], size)


def per_device(tokens_grad, expert_ids, combine_weights, gate_saved, up_saved, gate_weight, up_weight, down_weight):
    vmem = pl.BlockSpec(memory_space=pltpu.VMEM)
    hbm = pl.BlockSpec(memory_space=pl.ANY)
    dma = pltpu.SemaphoreType.DMA
    v = pltpu.VMEM
    scratch = [
        v((192, FD), BF16), v((2, 192), jnp.int32), v((2, 192), F32),
        v((640, HID), BF16), v((640, HID), BF16),
        v((3072, HID), BF16), v((3072, HID), BF16), v((HID, 3072), BF16),
        v((HID, NC), F32), v((HID, NC), F32),
        v((NE, 128, 192), BF16), v((NE, 192), F32), v((NE, 192), F32),
        v((NE, 64, 128), BF16), v((NE, 64, 128), BF16), v((NE, 64, 128), BF16), v((NE, 64, 128), BF16),
        v((NZ, SLAB, CA), BF16), v((NZ, SLAB, CB), BF16), v((NZ, HALF, CT), BF16), v((NZ, SLAB, CT), BF16),
        v((HID, NC), F32), v((HID, NC), BF16), v((HID, NC), BF16),
        v((NZ, SLAB, NC), F32),
        v((NZ, SLAB, CA), BF16), v((NZ, SLAB, CB), BF16), v((NZ, HALF, CT), BF16),
        v((4, SLAB, CA), BF16), v((4, SLAB, CA), BF16),
        v((NX, FD, CA), BF16), v((SLAB, CA), BF16),
        v((NZ, 3, FD, CB), BF16), v((NZ, 3, FD // 2, CT), BF16),
        v((NZ, FD, CB), BF16), v((NZ, FD // 2, CT), BF16),
        v((4, FD, CB), BF16), v((4, FD, CB), BF16), v((4, FD // 2, CT), BF16), v((4, FD // 2, CT), BF16),
        v((6720, 128), F32),
        dma((4,)), dma((8,)), dma((1,)), dma((1,)),
        dma((NX,)), dma((4, NX)), dma((4, NX)), dma((4,)), dma((3,)), dma((NZ, 3)),
        dma((4, NX)), dma((4, NX)), dma((NZ, 3)), dma((4,)), dma((4,)), dma((1,)),
    ]
    return pl.pallas_call(
        kernel,
        out_shape=pltpu.VMEM(tokens_grad.shape, BF16),
        in_specs=[hbm] * 8,
        out_specs=vmem,
        scratch_shapes=scratch,
        compiler_params=pltpu.CompilerParams(
            collective_id=0, has_side_effects=True, vmem_limit_bytes=60 * 2**20
        ),
        name="moe_backward",
    )(tokens_grad, expert_ids.T, combine_weights.T, gate_saved, up_saved, gate_weight, up_weight, down_weight)


def solution(mesh):
    in_specs = (
        P("expert", ("row", "col")),
        P("expert", None),
        P("expert", None),
        P("expert", None, ("row", "col")),
        P("expert", None, ("row", "col")),
        P("expert", None, ("row", "col")),
        P("expert", None, ("row", "col")),
        P("expert", ("row", "col"), None),
    )
    out_specs = P("expert", ("row", "col"))
    return jax.shard_map(
        per_device, mesh=mesh, in_specs=in_specs, out_specs=out_specs, check_vma=False
    )
```
